256 devices in a mesh: depth: 4 (over y), seg: 32 (over x, z), tp: 2 (over core).
Axes of the slice: x: 4, y: 4, z: 8, core: 2. Of those that a mesh axis runs over, the one named last changes fastest.
Arguments:
- queries: bfloat16 [16384, 8192], P(('depth', 'seg'), 'tp'), may hold values from -64 to 64
- key_states: bfloat16 [16384, 1024], P(('depth', 'seg'), 'tp'), may hold values from -6 to 6
- value_states: bfloat16 [16384, 1024], P(('depth', 'seg'), 'tp'), may hold values from -6 to 6
- grad_output: bfloat16 [16384, 8192], P(('depth', 'seg'), 'tp'), may hold values from -6 to 6
- parents: int32 [3, 32], replicated, may hold values from 0 to 31
- lengths: int32 [4, 32], replicated, may hold values from 1 to 128, 3072 in all within a row
Outputs:
- grad_queries: bfloat16 [16384, 8192], P(('depth', 'seg'), 'tp')
- grad_keys: bfloat16 [16384, 1024], P(('depth', 'seg'), 'tp')
- grad_values: bfloat16 [16384, 1024], P(('depth', 'seg'), 'tp')
The draws below stay inside these ranges and needn't reach their ends.
Inputs may be any that keep to these rules, and one draw needn't show every extreme that they name: parents[l, j] is the segment of level l that is the parent of segment j of level l + 1. lengths[l, s] is the number of live tokens of segment s of level l, the live ones first; in every level some segment has all 128.
All inputs are finite; a program needn't handle non-finite values.
Results may differ from the reference program's by a relative error of at most 0.011.
Values may be sent and summed in bfloat16 or wider, within the bound.
No kernel may reach another device: no remote copies, remote signals or barrier semaphores. Data moves between devices by JAX's collectives and lax.ppermute only.
A program may use at most 64 MiB of HBM per device.

```python
import math
import jax
import jax.numpy as jnp
import numpy as np
from jax import lax

HD = 128
SEGLEN = 128
LEVELS = 4
SEGS = 32
TOKENS = 16384
QF = 8192
KF = 1024


def bell_keys(key):
    return jnp.clip(jax.random.normal(jax.random.fold_in(key, 21), (TOKENS, KF), jnp.float32), -6.0, 6.0)


def draw_key_states(key, part):
    result = bell_keys(key)
    return result.astype(jnp.bfloat16)


def draw_queries(key, part):
    key = jax.random.fold_in(key, 2)
    result = jnp.clip(jax.random.normal(key, (TOKENS, QF), jnp.float32), -6.0, 6.0)
    return result.astype(jnp.bfloat16)


def touch_ends(drawn, stream_key, least, high):
    longest = drawn.shape.index(max(drawn.shape))
    spots = []
    for shift in (0, 1):
        where = [jax.random.randint(jax.random.fold_in(stream_key, axis), (), 0, length) for axis, length in enumerate(drawn.shape)]
        where[longest] = (where[longest] + shift) % drawn.shape[longest]
        spots.append(tuple(where))
    return drawn.at[spots[0]].set(least).at[spots[1]].set(high)


def block_levels(stream_key, dims, split, least, top_value):
    level, own = 1.0, jax.random.fold_in(stream_key, 6)
    for position, shards_of in split:
        draws = jnp.exp(jax.random.uniform(jax.random.fold_in(own, position), (shards_of,), jnp.float32, least / len(split), top_value / len(split)))
        level = level * jnp.repeat(draws, dims[position] // shards_of).reshape([-1 if axis == position else 1 for axis in range(len(dims))])
    return level


def profile(number_of, total, bound, skew):
    portions = [(1 << 20) // math.isqrt(grade ** skew) + 1 for grade in range(2, number_of + 1)]
    rest, holding = total - bound - (number_of - 1), [1] * (number_of - 1)
    while rest > 0:
        free = [i for i in range(number_of - 1) if holding[i] < bound]
        mass, budget = sum([portions[i] for i in free]), rest
        for i in free:
            addition = min(bound - holding[i], max(1, budget * portions[i] // mass), rest)
            holding[i] = holding[i] + addition
            rest = rest - addition
    return np.array([bound] + holding)


def ragged_sizes(rng, amount, total, reach, slope):
    if amount == 2:
        one = jax.random.randint(rng, (), max(1, total - reach), min(reach, total - 1) + 1)
        return jnp.stack([one, total - one])
    tallies = jnp.asarray(profile(amount, total, reach, slope), jnp.int32)
    couples = (amount - 1) // 2
    giver, sink = tallies[1:1 + 2 * couples:2], tallies[2:2 + 2 * couples:2]
    margin = jnp.minimum(giver - 1, reach - sink)
    moved = jax.random.randint(jax.random.fold_in(rng, 1), (couples,), 0, 1 << 20) % (margin + 1)
    tallies = tallies.at[1:1 + 2 * couples:2].set(giver - moved).at[2:2 + 2 * couples:2].set(sink + moved)
    return tallies[jax.random.permutation(jax.random.fold_in(rng, 2), amount)]


def gaussian(key, shape, scale, bound, split=(), kind=jnp.bfloat16):
    entries = jax.random.normal(key, shape, jnp.float32) * scale
    if len(split) > 0:
        entries = block_levels(key, shape, split, -0.22, 0.18) * entries
    return jnp.clip(entries, min=-bound, max=bound).astype(kind)


def setup_inputs(seed: int = 0) -> dict:
    splits = jax.random.split(jax.random.key(seed), 7)
    queries = draw_queries(jax.random.fold_in(splits[6], 71), 0)
    key_states = draw_key_states(jax.random.fold_in(splits[6], 71), 0)
    value_states = gaussian(splits[2], (TOKENS, KF), 1.0, 6.0, ((0, 128), (1, 2)))
    grad_output = gaussian(splits[3], (TOKENS, QF), 1.0, 6.0, ((0, 128), (1, 2)))
    parents = touch_ends(jax.random.randint(splits[4], (LEVELS - 1, SEGS), 0, SEGS), jax.random.fold_in(splits[4], 1), 0, SEGS - 1).astype(jnp.int32)
    lengths = jax.vmap(lambda own: ragged_sizes(own, SEGS, SEGS * SEGLEN * 3 // 4, SEGLEN, 1))(jax.random.split(splits[5], LEVELS)).reshape((LEVELS, SEGS)).astype(jnp.int32)
    return dict(queries=queries, key_states=key_states, value_states=value_states, grad_output=grad_output, parents=parents, lengths=lengths)


def lookup(table_row, index):
    slots = jnp.arange(table_row.shape[0], dtype=jnp.int32)
    picked = jnp.where(index[:, None] == slots[None, :], table_row[None, :], 0)
    return lax.optimization_barrier(jnp.sum(picked, axis=1)).astype(jnp.int32)

def ancestor_table(parents, levels):
    segments = parents.shape[1]
    anchor = jnp.arange(segments, dtype=jnp.int32)
    layers = []
    for depth_level in range(levels):
        column = [jnp.zeros((segments,), jnp.int32) for other in range(levels)]
        current = anchor
        column[depth_level] = current
        for upper_level in range(depth_level - 1, -1, -1):
            current = lookup(parents[upper_level], current)
            column[upper_level] = current
        layers.append(jnp.stack(column))
    return jnp.stack(layers)

def attention_grad(queries, grad_output, key_states, value_states, allowed, live_rows):
    row_count = queries.shape[0]
    group_count = key_states.shape[1] // HD
    repeat_count = queries.shape[1] // key_states.shape[1]
    factor = HD ** (-0.5)
    grad_live = jnp.where(live_rows[:, None], grad_output, jnp.zeros_like(grad_output))
    query_parts, key_parts, value_parts = ([], [], [])
    for group_index in range(group_count):
        low = group_index * repeat_count * HD
        high = low + repeat_count * HD
        query_block = queries[:, low:high].reshape(row_count, repeat_count, HD).astype(jnp.float32)
        grad_block = grad_live[:, low:high].reshape(row_count, repeat_count, HD).astype(jnp.float32)
        key_block = key_states[:, group_index * HD:(group_index + 1) * HD].astype(jnp.float32)
        value_block = value_states[:, group_index * HD:(group_index + 1) * HD].astype(jnp.float32)
        scores = jnp.einsum('reh,lh->erl', query_block, key_block) * factor
        scores = jnp.where(allowed[None], scores, -jnp.inf)
        highest = lax.optimization_barrier(jnp.max(scores, axis=2, keepdims=True))
        weights = jnp.exp(scores - highest)
        softmax_weights = weights / lax.optimization_barrier(jnp.sum(weights, axis=2, keepdims=True))
        probs_low = softmax_weights.astype(jnp.bfloat16)
        probs_wide = probs_low.astype(jnp.float32)
        attended = jnp.einsum('erl,lh->reh', probs_wide, value_block)
        correction = jnp.transpose(lax.optimization_barrier(jnp.sum(grad_block * attended, axis=2)))
        grad_probs = jnp.einsum('reh,lh->erl', grad_block, value_block)
        grad_scores = (softmax_weights * (grad_probs - correction[:, :, None]) * factor).astype(jnp.bfloat16)
        grad_wide = grad_scores.astype(jnp.float32)
        query_parts.append(jnp.einsum('erl,lh->reh', grad_wide, key_block).reshape(row_count, repeat_count * HD))
        key_parts.append(jnp.einsum('erl,reh->lh', grad_wide, query_block))
        value_parts.append(jnp.einsum('erl,reh->lh', probs_wide, grad_block))
    return (jnp.concatenate(query_parts, axis=1), jnp.concatenate(key_parts, axis=1), jnp.concatenate(value_parts, axis=1))

def reference(queries, key_states, value_states, grad_output, parents, lengths):
    table = ancestor_table(parents, LEVELS)
    positions = jnp.arange(SEGLEN, dtype=jnp.int32)
    level_ids = jnp.arange(LEVELS, dtype=jnp.int32)
    segment_ids = jnp.arange(SEGS, dtype=jnp.int32)

    def per_segment(carry, flat_index):
        total_keys, total_values = carry
        level_here = (flat_index // SEGS).astype(jnp.int32)
        seg_here = (flat_index % SEGS).astype(jnp.int32)
        chain_here = lax.dynamic_index_in_dim(table, level_here, 0, keepdims=False)
        ancestors_here = lax.dynamic_index_in_dim(chain_here, seg_here, 1, keepdims=False)
        block_lengths = lax.optimization_barrier(jnp.sum(jnp.where(ancestors_here[:, None] == segment_ids[None, :], lengths, 0), axis=1))
        own_length = lax.dynamic_index_in_dim(block_lengths, level_here, 0, keepdims=False)
        offsets = ((level_ids * SEGS + ancestors_here) * SEGLEN).astype(jnp.int32)
        key_list = jnp.concatenate([lax.dynamic_slice_in_dim(key_states, offsets[level], SEGLEN, 0) for level in range(LEVELS)], axis=0)
        value_list = jnp.concatenate([lax.dynamic_slice_in_dim(value_states, offsets[level], SEGLEN, 0) for level in range(LEVELS)], axis=0)
        below = (level_ids < level_here)[None, :, None] & (positions[None, None, :] < block_lengths[None, :, None])
        own_part = (level_ids == level_here)[None, :, None] & (positions[None, None, :] <= positions[:, None, None]) & (positions[None, None, :] < own_length)
        allowed = (below | own_part).reshape(SEGLEN, LEVELS * SEGLEN)
        live_rows = positions < own_length
        first_row = (flat_index * SEGLEN).astype(jnp.int32)
        query_rows = lax.dynamic_slice_in_dim(queries, first_row, SEGLEN, 0)
        grad_rows = lax.dynamic_slice_in_dim(grad_output, first_row, SEGLEN, 0)
        grad_q, grad_k, grad_v = attention_grad(query_rows, grad_rows, key_list, value_list, allowed, live_rows)
        for level in range(LEVELS):
            term_keys = grad_k[level * SEGLEN:(level + 1) * SEGLEN]
            term_values = grad_v[level * SEGLEN:(level + 1) * SEGLEN]
            round_keys, round_values = lax.optimization_barrier((term_keys.astype(jnp.bfloat16), term_values.astype(jnp.bfloat16)))
            term_keys = jnp.where(level < level_here, round_keys.astype(jnp.float32), term_keys)
            term_values = jnp.where(level < level_here, round_values.astype(jnp.float32), term_values)
            old_keys = lax.dynamic_slice_in_dim(total_keys, offsets[level], SEGLEN, 0)
            old_values = lax.dynamic_slice_in_dim(total_values, offsets[level], SEGLEN, 0)
            total_keys = lax.dynamic_update_slice_in_dim(total_keys, old_keys + term_keys, offsets[level], 0)
            total_values = lax.dynamic_update_slice_in_dim(total_values, old_values + term_values, offsets[level], 0)
        return ((total_keys, total_values), grad_q.astype(jnp.bfloat16))
    start_keys = jnp.zeros((TOKENS, KF), jnp.float32)
    start_values = jnp.zeros((TOKENS, KF), jnp.float32)
    (total_keys, total_values), grad_q = lax.scan(per_segment, (start_keys, start_values), jnp.arange(LEVELS * SEGS, dtype=jnp.int32))
    return (grad_q.reshape(TOKENS, QF), total_keys.astype(jnp.bfloat16), total_values.astype(jnp.bfloat16))
```

```python
import functools

import jax
import jax.numpy as jnp
from jax import lax
from jax.experimental import pallas as pl
from jax.experimental.pallas import tpu as pltpu
from jax.sharding import PartitionSpec as P

HD = 128
LEVELS = 4
SEGS = 32
ROWS = 128
HEADS = 4
REPEAT = 8
TILES = 2 * HEADS
UPPER = LEVELS - 1
DEVICES = LEVELS * SEGS
LOG2E = 1.4426950408889634
FACTOR = HD ** (-0.5)
VMEM = pl.BlockSpec(memory_space=pltpu.VMEM)
SMEM = pl.BlockSpec(memory_space=pltpu.SMEM)


def params():
    return pltpu.CompilerParams(vmem_limit_bytes=48 * 1024 * 1024)


def pack_kernel(key_ref, value_ref, out_ref, wide):
    for head in range(HEADS):
        lanes = slice(head * HD, (head + 1) * HD)
        wide[pl.ds(head, ROWS, stride=TILES), :] = key_ref[:, lanes].astype(jnp.float32)
        wide[pl.ds(HEADS + head, ROWS, stride=TILES), :] = value_ref[:, lanes].astype(jnp.float32)
    out_ref[...] = wide[...].reshape(ROWS, TILES, HD).astype(jnp.bfloat16)


def pack(keys, values):
    return pl.pallas_call(
        pack_kernel,
        out_shape=jax.ShapeDtypeStruct((ROWS, TILES, HD), jnp.bfloat16),
        in_specs=[VMEM, VMEM],
        out_specs=VMEM,
        scratch_shapes=[pltpu.VMEM((ROWS * TILES, HD), jnp.float32)],
        compiler_params=params(),
    )(keys, values)


def chains(parents_ref, seg):
    found = []
    for level in range(1, LEVELS):
        current = seg
        for upper in range(level - 1, -1, -1):
            current = parents_ref[upper, current]
            found.append((level, upper, current))
    return found


def select_kernel(parents_ref, held_ref, out_ref):
    out_ref[0:SEGS] = jnp.zeros((SEGS, UPPER, TILES, HD), jnp.bfloat16)
    blank = jnp.zeros((TILES, HD), jnp.bfloat16)

    def step(seg, carry):
        for level, upper, ancestor in chains(parents_ref, seg):
            out_ref[level * SEGS + seg, upper] = held_ref[upper * SEGS + ancestor]
        for level in range(1, UPPER):
            for upper in range(level, UPPER):
                out_ref[level * SEGS + seg, upper] = blank
        return carry

    lax.fori_loop(0, SEGS, step, 0, unroll=8)


def select(parents, held):
    return pl.pallas_call(
        select_kernel,
        out_shape=jax.ShapeDtypeStruct((DEVICES, UPPER, TILES, HD), jnp.bfloat16),
        in_specs=[SMEM, VMEM],
        out_specs=VMEM,
        compiler_params=params(),
    )(parents, held)


def sum_kernel(parents_ref, terms_ref, out_ref, total):
    total[...] = jnp.zeros_like(total)

    def step(seg, carry):
        for level, upper, ancestor in chains(parents_ref, seg):
            total[upper * SEGS + ancestor] += terms_ref[level * SEGS + seg, upper].astype(jnp.float32)
        return carry

    lax.fori_loop(0, SEGS, step, 0, unroll=8)
    out_ref[0 : UPPER * SEGS] = total[...].astype(jnp.bfloat16)
    out_ref[UPPER * SEGS :] = jnp.zeros((SEGS, TILES, HD), jnp.bfloat16)


def sum_terms(parents, terms):
    return pl.pallas_call(
        sum_kernel,
        out_shape=jax.ShapeDtypeStruct((DEVICES, TILES, HD), jnp.bfloat16),
        in_specs=[SMEM, VMEM],
        out_specs=VMEM,
        scratch_shapes=[pltpu.VMEM((UPPER * SEGS, TILES, HD), jnp.float32)],
        compiler_params=params(),
    )(parents, terms)


def dot_last(left, right):
    return lax.dot_general(left, right, (((1,), (1,)), ((), ())), preferred_element_type=jnp.float32)


def dot(left, right):
    return jnp.dot(left, right, preferred_element_type=jnp.float32)


def attention_kernel(
    place_ref, parents_ref, lengths_ref,
    query_ref, grad_ref, key_ref, value_ref, held_ref,
    gquery_ref, own_key_ref, own_value_ref, terms_ref,
    bias, wide, sums,
):
    head = pl.program_id(0)
    level = place_ref[0]
    seg = place_ref[1]
    own_length = lengths_ref[level, seg]

    @pl.when(head == 0)
    def _():
        slots = lax.broadcasted_iota(jnp.int32, (ROWS, ROWS), 0)
        rows = lax.broadcasted_iota(jnp.int32, (ROWS, ROWS), 1)
        never = jnp.full((ROWS, ROWS), -jnp.inf, jnp.float32)
        current = seg
        for upper in range(UPPER - 1, -1, -1):
            below = upper < level
            current = jnp.where(below, parents_ref[upper, current], current)
            live = jnp.where(below, lengths_ref[upper, current], 0)
            bias[upper * ROWS : (upper + 1) * ROWS, :] = jnp.where(slots < live, 0.0, never)
            wide[upper] = held_ref[:, upper].astype(jnp.float32).reshape(ROWS * TILES, HD)
        allowed = (slots <= rows) & (slots < own_length)
        bias[UPPER * ROWS :, :] = jnp.where(allowed, 0.0, never)

    keys = jnp.concatenate(
        [wide[u, pl.ds(head, ROWS, stride=TILES), :].astype(jnp.bfloat16) for u in range(UPPER)] + [key_ref[...]]
    )
    values = jnp.concatenate(
        [wide[u, pl.ds(HEADS + head, ROWS, stride=TILES), :].astype(jnp.bfloat16) for u in range(UPPER)]
        + [value_ref[...]]
    )
    keys_turned = keys.T
    live_rows = lax.broadcasted_iota(jnp.int32, (ROWS, HD), 0) < own_length
    blocked = bias[...]
    key_sum = jnp.zeros((LEVELS * ROWS, HD), jnp.float32)
    value_sum = jnp.zeros((LEVELS * ROWS, HD), jnp.float32)
    for pair in range(REPEAT // 2):
        heads = [slice((2 * pair + i) * HD, (2 * pair + i + 1) * HD) for i in range(2)]
        query = jnp.concatenate([query_ref[:, lanes] for lanes in heads])
        grad = jnp.concatenate(
            [jnp.where(live_rows, grad_ref[:, lanes], jnp.zeros((), jnp.bfloat16)) for lanes in heads]
        )
        scores = dot_last(keys, query) * (FACTOR * LOG2E) + jnp.concatenate([blocked, blocked], axis=1)
        weights = jnp.exp2(scores - jnp.max(scores, axis=0, keepdims=True))
        inverse = 1.0 / jnp.sum(weights, axis=0, keepdims=True)
        probs = weights * inverse
        grad_probs = dot_last(values, grad)
        correction = jnp.sum(probs * grad_probs, axis=0, keepdims=True)
        grad_scores = (probs * ((grad_probs - correction) * FACTOR)).astype(jnp.bfloat16)
        value_sum += dot(probs.astype(jnp.bfloat16), grad)
        key_sum += dot(grad_scores, query)
        turned = dot(keys_turned, grad_scores).astype(jnp.bfloat16)
        for i, lanes in enumerate(heads):
            gquery_ref[:, lanes] = turned[:, i * ROWS : (i + 1) * ROWS].T
    own_key_ref[...] = key_sum[UPPER * ROWS :]
    own_value_ref[...] = value_sum[UPPER * ROWS :]
    for upper in range(UPPER):
        block = slice(upper * ROWS, (upper + 1) * ROWS)
        sums[upper, pl.ds(head, ROWS, stride=TILES), :] = key_sum[block]
        sums[upper, pl.ds(HEADS + head, ROWS, stride=TILES), :] = value_sum[block]

    @pl.when(head == HEADS - 1)
    def _():
        for upper in range(UPPER):
            terms_ref[:, upper] = sums[upper].reshape(ROWS, TILES, HD).astype(jnp.bfloat16)


def attention(place, parents, lengths, queries, grad_output, keys, values, held):
    wide_block = pl.BlockSpec((ROWS, REPEAT * HD), lambda h: (0, h))
    head_block = pl.BlockSpec((ROWS, HD), lambda h: (0, h))
    held_block = pl.BlockSpec((ROWS, UPPER, TILES, HD), lambda h: (0, 0, 0, 0))
    width = HEADS * HD
    return pl.pallas_call(
        attention_kernel,
        grid=(HEADS,),
        out_shape=(
            jax.ShapeDtypeStruct((ROWS, REPEAT * width), jnp.bfloat16),
            jax.ShapeDtypeStruct((ROWS, width), jnp.float32),
            jax.ShapeDtypeStruct((ROWS, width), jnp.float32),
            jax.ShapeDtypeStruct((ROWS, UPPER, TILES, HD), jnp.bfloat16),
        ),
        in_specs=[SMEM, SMEM, SMEM, wide_block, wide_block, head_block, head_block, held_block],
        out_specs=(wide_block, head_block, head_block, held_block),
        scratch_shapes=[
            pltpu.VMEM((LEVELS * ROWS, ROWS), jnp.float32),
            pltpu.VMEM((UPPER, ROWS * TILES, HD), jnp.float32),
            pltpu.VMEM((UPPER, ROWS * TILES, HD), jnp.float32),
        ],
        compiler_params=params(),
    )(place, parents, lengths, queries, grad_output, keys, values, held)


def finish_kernel(extra_ref, own_key_ref, own_value_ref, key_ref, value_ref, wide):
    wide[...] = extra_ref[...].astype(jnp.float32).reshape(ROWS * TILES, HD)
    for head in range(HEADS):
        lanes = slice(head * HD, (head + 1) * HD)
        extra_key = wide[pl.ds(head, ROWS, stride=TILES), :]
        extra_value = wide[pl.ds(HEADS + head, ROWS, stride=TILES), :]
        key_ref[:, lanes] = (own_key_ref[:, lanes] + extra_key).astype(jnp.bfloat16)
        value_ref[:, lanes] = (own_value_ref[:, lanes] + extra_value).astype(jnp.bfloat16)


def finish(extra, own_keys, own_values):
    shape = jax.ShapeDtypeStruct((ROWS, HEADS * HD), jnp.bfloat16)
    return pl.pallas_call(
        finish_kernel,
        out_shape=(shape, shape),
        in_specs=[VMEM] * 3,
        out_specs=(VMEM, VMEM),
        scratch_shapes=[pltpu.VMEM((ROWS * TILES, HD), jnp.float32)],
        compiler_params=params(),
    )(extra, own_keys, own_values)


def exchange(pieces):
    return lax.all_to_all(pieces, ("depth", "seg"), 0, 0, tiled=True)


def per_device(queries, key_states, value_states, grad_output, parents, lengths):
    place = jnp.stack([lax.axis_index("depth"), lax.axis_index("seg")]).astype(jnp.int32)
    held = exchange(pack(key_states, value_states))
    arrived = exchange(select(parents, held))
    grad_q, own_keys, own_values, terms = attention(
        place, parents, lengths, queries, grad_output, key_states, value_states, arrived
    )
    extra = exchange(sum_terms(parents, exchange(terms)))
    grad_k, grad_v = finish(extra, own_keys, own_values)
    return grad_q, grad_k, grad_v


def solution(mesh):
    placed = P(("depth", "seg"), "tp")
    return jax.shard_map(
        per_device,
        mesh=mesh,
        in_specs=(placed, placed, placed, placed, P(), P()),
        out_specs=(placed, placed, placed),
        check_vma=False,
    )
```

```python
import jax
import jax.numpy as jnp
from jax import lax
from jax.experimental import pallas as pl
from jax.experimental.pallas import tpu as pltpu
from jax.sharding import PartitionSpec as P

HD = 128
LEVELS = 4
SEGS = 32
ROWS = 128
HEADS = 4
REPEAT = 8
GROUP = REPEAT * HD
WIDTH = HEADS * HD
TILE = 2 * HEADS
UPPER = LEVELS - 1
DEVICES = LEVELS * SEGS
SLOTS = 6
PIECE = 2 * SLOTS
HALF = HEADS // 2
GUEST_GRAD = HALF * GROUP
GUEST_KEY = 2 * HALF * GROUP
GUEST_VALUE = GUEST_KEY + HALF * HD
BACK_KEY = HALF * GROUP
BACK_VALUE = BACK_KEY + HALF * HD
LOG2E = 1.4426950408889634
FACTOR = HD ** (-0.5)
VMEM = pl.BlockSpec(memory_space=pltpu.VMEM)
SMEM = pl.BlockSpec(memory_space=pltpu.SMEM)

TASKS = {
    0: ((True, 2, (0, 2, 4)), (True, 3, (1, 3, 5))),
    1: ((False, 0, (0,)), (False, 1, (1,)), (False, 2, (2,)), (False, 3, (3,)), (True, 3, (4, 5))),
    2: ((False, 0, (0, 2)), (False, 1, (1, 3)), (False, 2, (4, 5))),
    3: ((False, 0, (0, 2, 4)), (False, 1, (1, 3, 5))),
}
HOST = {0: 3, 1: 2}


def call(kernel, out_shape, in_specs, out_specs, scratch=(), flops=0, moved=0, grid=None):
    extra = {} if grid is None else {"grid": grid}
    return pl.pallas_call(
        kernel,
        out_shape=out_shape,
        in_specs=in_specs,
        out_specs=out_specs,
        scratch_shapes=list(scratch),
        cost_estimate=pl.CostEstimate(flops=flops, bytes_accessed=moved, transcendentals=0),
        compiler_params=pltpu.CompilerParams(vmem_limit_bytes=48 * 1024 * 1024),
        **extra,
    )


def low(*shape):
    return jax.ShapeDtypeStruct(shape, jnp.bfloat16)


def full(*shape):
    return jax.ShapeDtypeStruct(shape, jnp.float32)


def wide_scratch(rows):
    return pltpu.VMEM((rows, HD), jnp.float32)


def pack_kernel(key_ref, value_ref, out_ref, wide):
    for head in range(HEADS):
        lanes = slice(head * HD, (head + 1) * HD)
        wide[pl.ds(2 * head, ROWS, stride=TILE), :] = key_ref[:, lanes].astype(jnp.float32)
        wide[pl.ds(2 * head + 1, ROWS, stride=TILE), :] = value_ref[:, lanes].astype(jnp.float32)
    out_ref[...] = wide[...].astype(jnp.bfloat16)


def pack(keys, values):
    return call(pack_kernel, low(ROWS * TILE, HD), [VMEM, VMEM], VMEM, [wide_scratch(ROWS * TILE)])(keys, values)


def chain(parents_ref, level, seg):
    found = []
    current = seg
    for upper in range(level - 1, -1, -1):
        current = parents_ref[upper, current]
        found.insert(0, current)
    return found


def tile_at(upper, ancestor):
    return pl.ds(pl.multiple_of((upper * SEGS + ancestor) * TILE, TILE), TILE)


def rows_of(level, seg, first, count):
    return pl.ds((level * SEGS + seg) * PIECE + first, count)


def select_kernel(parents_ref, held_ref, out_ref, wide, picked):
    wide[...] = held_ref[...].astype(jnp.float32)

    def step(seg, carry):
        for upper, ancestor in enumerate(chain(parents_ref, 3, seg)):
            tile = wide[tile_at(upper, ancestor), :]
            picked[rows_of(3, seg, 4 * upper, 4), :] = tile[0:4]
            picked[rows_of(0, seg, 4 * upper, 4), :] = tile[4:8]
        first, second = [wide[tile_at(u, a), :] for u, a in enumerate(chain(parents_ref, 2, seg))]
        picked[rows_of(2, seg, 0, 4), :] = first[0:4]
        picked[rows_of(2, seg, 4, 4), :] = second[0:4]
        picked[rows_of(2, seg, 8, 2), :] = first[4:6]
        picked[rows_of(2, seg, 10, 2), :] = second[4:6]
        picked[rows_of(1, seg, 8, 2), :] = first[6:8]
        picked[rows_of(1, seg, 10, 2), :] = second[6:8]
        (only,) = chain(parents_ref, 1, seg)
        picked[rows_of(1, seg, 0, 8), :] = wide[tile_at(0, only), :]
        return carry

    lax.fori_loop(0, SEGS, step, 0, unroll=8)
    out_ref[...] = picked[...].astype(jnp.bfloat16)


def select(parents, held):
    scratch = [wide_scratch(DEVICES * TILE), wide_scratch(DEVICES * PIECE)]
    return call(select_kernel, low(DEVICES * PIECE, HD), [SMEM, VMEM], VMEM, scratch)(parents, held)


def sum_kernel(parents_ref, terms_ref, out_ref, wide, total):
    wide[...] = terms_ref[...].astype(jnp.float32)
    total[...] = jnp.zeros_like(total)

    def rows(level, seg, first, count):
        return wide[rows_of(level, seg, first, count), :]

    def step(seg, carry):
        for upper, ancestor in enumerate(chain(parents_ref, 3, seg)):
            total[tile_at(upper, ancestor), :] += jnp.concatenate(
                [rows(3, seg, 4 * upper, 4), rows(0, seg, 4 * upper, 4)]
            )
        for upper, ancestor in enumerate(chain(parents_ref, 2, seg)):
            total[tile_at(upper, ancestor), :] += jnp.concatenate(
                [rows(2, seg, 4 * upper, 4), rows(2, seg, 8 + 2 * upper, 2), rows(1, seg, 8 + 2 * upper, 2)]
            )
        (only,) = chain(parents_ref, 1, seg)
        total[tile_at(0, only), :] += rows(1, seg, 0, 8)
        return carry

    lax.fori_loop(0, SEGS, step, 0, unroll=8)
    used = UPPER * SEGS * TILE
    out_ref[0:used] = total[...].astype(jnp.bfloat16)
    out_ref[used:] = jnp.zeros((SEGS * TILE, HD), jnp.bfloat16)


def sum_terms(parents, terms):
    scratch = [wide_scratch(DEVICES * PIECE), wide_scratch(UPPER * SEGS * TILE)]
    return call(sum_kernel, low(DEVICES * TILE, HD), [SMEM, VMEM], VMEM, scratch)(parents, terms)


def dot_last(left, right):
    return lax.dot_general(left, right, (((1,), (1,)), ((), ())), preferred_element_type=jnp.float32)


def dot(left, right):
    return jnp.dot(left, right, preferred_element_type=jnp.float32)


def block_mask(lengths):
    slots = lax.broadcasted_iota(jnp.int32, (ROWS, ROWS), 0)
    rows = lax.broadcasted_iota(jnp.int32, (ROWS, ROWS), 1)
    allowed = [slots < length for length in lengths]
    allowed[-1] = allowed[-1] & (slots <= rows)
    return jnp.concatenate([jnp.where(each, 0.0, -jnp.inf).astype(jnp.float32) for each in allowed])


def head_grad(keys, values, blocked, live_rows, query_at, grad_at, store):
    query = jnp.concatenate([query_at(i) for i in range(REPEAT)])
    grad = jnp.concatenate(
        [jnp.where(live_rows, grad_at(i), jnp.zeros((), jnp.bfloat16)) for i in range(REPEAT)]
    )
    scores = dot_last(keys, query) * (FACTOR * LOG2E) + jnp.concatenate([blocked] * REPEAT, axis=1)
    weights = jnp.exp2(scores - jnp.max(scores, axis=0, keepdims=True))
    probs = weights * (1.0 / jnp.sum(weights, axis=0, keepdims=True))
    grad_probs = dot_last(values, grad)
    correction = jnp.sum(probs * grad_probs, axis=0, keepdims=True)
    grad_scores = (probs * ((grad_probs - correction) * FACTOR)).astype(jnp.bfloat16)
    value_sum = dot(probs.astype(jnp.bfloat16), grad)
    key_sum = dot(grad_scores, query)
    turned = dot(keys.T, grad_scores).astype(jnp.bfloat16)
    for i in range(REPEAT):
        store(i, turned[:, i * ROWS : (i + 1) * ROWS].T)
    return key_sum, value_sum


def live(length):
    return lax.broadcasted_iota(jnp.int32, (ROWS, HD), 0) < length


def lanes_at(ref, start, width=HD):
    return ref.at[:, start : start + width]


def root_kernel(place_ref, lengths_ref, query_ref, grad_ref, key_ref, value_ref, gquery_ref, gkey_ref, gvalue_ref):
    @pl.when(place_ref[0] == 0)
    def _():
        length = lengths_ref[0, place_ref[1]]
        blocked = block_mask([length])
        for head in range(HEADS):
            lanes = slice(head * HD, (head + 1) * HD)

            def store(i, block):
                lanes_at(gquery_ref, head * GROUP + i * HD)[...] = block

            gkey_ref[:, lanes], gvalue_ref[:, lanes] = head_grad(
                key_ref[:, lanes],
                value_ref[:, lanes],
                blocked,
                live(length),
                lambda i: lanes_at(query_ref, head * GROUP + i * HD)[...],
                lambda i: lanes_at(grad_ref, head * GROUP + i * HD)[...],
                store,
            )


def root_grad(place, lengths, queries, grad_output, keys, values):
    shapes = (low(ROWS, HEADS * GROUP), full(ROWS, WIDTH), full(ROWS, WIDTH))
    specs = [SMEM, SMEM] + [VMEM] * 4
    return call(root_kernel, shapes, specs, (VMEM,) * 3, flops=10**9, moved=6 * 2**20)(
        place, lengths, queries, grad_output, keys, values
    )


def attention_kernel(
    place_ref, parents_ref, lengths_ref,
    query_ref, grad_ref, key_ref, value_ref, guest_ref, held_ref,
    gquery_ref, gkey_ref, gvalue_ref, back_ref, terms_ref,
    wide, sums,
):
    seg = place_ref[1]
    wide[...] = held_ref[...].astype(jnp.float32)

    def slot_rows(slot, part):
        return pl.ds(2 * slot + part, ROWS, stride=PIECE)

    def run(level_here):
        def setting(level):
            lengths = [lengths_ref[u, a] for u, a in enumerate(chain(parents_ref, level, seg))]
            lengths.append(lengths_ref[level, seg])
            return block_mask(lengths), live(lengths[-1])

        own = setting(level_here) if level_here else None
        hosted = setting(HOST[level_here]) if level_here in HOST else None
        for guest, head, slots in TASKS[level_here]:
            if guest:
                place = head - HALF
                sources = (guest_ref, place * GROUP, guest_ref, GUEST_GRAD + place * GROUP)
                own_key = lanes_at(guest_ref, GUEST_KEY + place * HD)
                own_value = lanes_at(guest_ref, GUEST_VALUE + place * HD)
                target, first = back_ref, place * GROUP
                key_target = lanes_at(back_ref, BACK_KEY + place * HD)
                value_target = lanes_at(back_ref, BACK_VALUE + place * HD)
            else:
                sources = (query_ref, head * GROUP, grad_ref, head * GROUP)
                own_key, own_value = lanes_at(key_ref, head * HD), lanes_at(value_ref, head * HD)
                target, first = gquery_ref, head * GROUP
                key_target, value_target = lanes_at(gkey_ref, head * HD), lanes_at(gvalue_ref, head * HD)
            blocked, live_rows = hosted if guest else own
            keys, values = [
                jnp.concatenate(
                    [wide[slot_rows(slot, part), :].astype(jnp.bfloat16) for slot in slots] + [mine[...]]
                )
                for part, mine in enumerate((own_key, own_value))
            ]

            def store(i, block):
                lanes_at(target, first + i * HD)[...] = block

            key_sum, value_sum = head_grad(
                keys,
                values,
                blocked,
                live_rows,
                lambda i: lanes_at(sources[0], sources[1] + i * HD)[...],
                lambda i: lanes_at(sources[2], sources[3] + i * HD)[...],
                store,
            )
            for index, slot in enumerate(slots):
                block = slice(index * ROWS, (index + 1) * ROWS)
                sums[slot_rows(slot, 0), :] = key_sum[block]
                sums[slot_rows(slot, 1), :] = value_sum[block]
            key_target[...] = key_sum[len(slots) * ROWS :].astype(key_target.dtype)
            value_target[...] = value_sum[len(slots) * ROWS :].astype(value_target.dtype)

    for level in range(LEVELS):
        pl.when(place_ref[0] == level)(lambda level=level: run(level))
    terms_ref[...] = sums[...].astype(jnp.bfloat16)


def attention(place, parents, lengths, queries, grad_output, keys, values, guest, held):
    shapes = (
        low(ROWS, HEADS * GROUP), full(ROWS, WIDTH), full(ROWS, WIDTH),
        low(ROWS, BACK_VALUE + HALF * HD), low(ROWS * PIECE, HD),
    )
    specs = [SMEM] * 3 + [VMEM] * 6
    scratch = [wide_scratch(ROWS * PIECE), wide_scratch(ROWS * PIECE)]
    return call(attention_kernel, shapes, specs, (VMEM,) * 5, scratch, flops=3 * 10**9, moved=10 * 2**20)(
        place, parents, lengths, queries, grad_output, keys, values, guest, held
    )


def join_kernel(place_ref, root_ref, here_ref, back_ref, out_ref):
    level = place_ref[0]
    head = pl.program_id(0)
    away = ((level == 3) & (head >= HALF)) | ((level == 2) & (head == HEADS - 1))

    @pl.when(away)
    def _():
        out_ref[...] = back_ref[...]

    @pl.when(level == 0)
    def _():
        out_ref[...] = root_ref[...]

    @pl.when((level != 0) & jnp.logical_not(away))
    def _():
        out_ref[...] = here_ref[...]


def join(place, root, here, back):
    block = pl.BlockSpec((ROWS, GROUP), lambda h: (0, h))
    late = pl.BlockSpec((ROWS, GROUP), lambda h: (0, jnp.maximum(h - HALF, 0)))
    return call(
        join_kernel, low(ROWS, HEADS * GROUP), [SMEM, block, block, late], block, grid=(HEADS,), moved=4 * 2**20
    )(place, root, here, back)


def finish_kernel(
    place_ref, extra_ref, root_key_ref, root_value_ref, here_key_ref, here_value_ref, back_ref, key_ref, value_ref, wide
):
    level = place_ref[0]
    wide[...] = extra_ref[...].astype(jnp.float32)
    for head in range(HEADS):
        lanes = slice(head * HD, (head + 1) * HD)
        away = ((level == 3) & (head >= HALF)) | ((level == 2) & (head == HEADS - 1))
        parts = (
            (root_key_ref, here_key_ref, BACK_KEY, key_ref),
            (root_value_ref, here_value_ref, BACK_VALUE, value_ref),
        )
        for part, (root_ref, here_ref, start, out_ref) in enumerate(parts):
            own = jnp.where(level == 0, root_ref[:, lanes], here_ref[:, lanes])
            if head >= HALF:
                back = back_ref[:, start + (head - HALF) * HD : start + (head - HALF + 1) * HD]
                own = jnp.where(away, back.astype(jnp.float32), own)
            out_ref[:, lanes] = (own + wide[pl.ds(2 * head + part, ROWS, stride=TILE), :]).astype(jnp.bfloat16)


def finish(place, extra, root_key, root_value, here_key, here_value, back):
    shapes = (low(ROWS, WIDTH), low(ROWS, WIDTH))
    specs = [SMEM] + [VMEM] * 6
    return call(finish_kernel, shapes, specs, (VMEM, VMEM), [wide_scratch(ROWS * TILE)])(
        place, extra, root_key, root_value, here_key, here_value, back
    )


def exchange(pieces, *tile):
    rows = pieces.shape[0]
    swapped = lax.all_to_all(pieces.reshape(DEVICES, *tile, HD), ("depth", "seg"), 0, 0, tiled=True)
    return swapped.reshape(rows, HD)


def per_device(queries, key_states, value_states, grad_output, parents, lengths):
    place = jnp.stack([lax.axis_index("depth"), lax.axis_index("seg")]).astype(jnp.int32)
    held = exchange(pack(key_states, value_states), TILE)
    lent = jnp.concatenate(
        [queries[:, HALF * GROUP :], grad_output[:, HALF * GROUP :], key_states[:, HALF * HD :], value_states[:, HALF * HD :]],
        axis=1,
    )
    guest = lax.ppermute(lent, "depth", [(host, here) for here, host in HOST.items()])
    root_q, root_k, root_v = root_grad(place, lengths, queries, grad_output, key_states, value_states)
    arrived = exchange(select(parents, held), SLOTS // 2, 4)
    here_q, here_k, here_v, back, terms = attention(
        place, parents, lengths, queries, grad_output, key_states, value_states, guest, arrived
    )
    back = lax.ppermute(back, "depth", list(HOST.items()))
    grad_q = join(place, root_q, here_q, back)
    extra = exchange(sum_terms(parents, exchange(terms, SLOTS // 2, 4)), TILE)
    grad_k, grad_v = finish(place, extra, root_k, root_v, here_k, here_v, back)
    return grad_q, grad_k, grad_v


def solution(mesh):
    placed = P(("depth", "seg"), "tp")
    return jax.shard_map(
        per_device,
        mesh=mesh,
        in_specs=(placed, placed, placed, placed, P(), P()),
        out_specs=(placed, placed, placed),
        check_vma=False,
    )
```

```python
import jax
import jax.numpy as jnp
from jax import lax
from jax.experimental import pallas as pl
from jax.experimental.pallas import tpu as pltpu
from jax.sharding import PartitionSpec as P

HD = 128
LEVELS = 4
SEGS = 32
ROWS = 128
HEADS = 4
REPEAT = 8
GROUP = REPEAT * HD
WIDTH = HEADS * HD
TILE = 2 * HEADS
UPPER = LEVELS - 1
DEVICES = LEVELS * SEGS
SLOTS = 6
PIECE = 2 * SLOTS
HALF = HEADS // 2
LENT = HALF * (GROUP + HD)
BACK_KEY = HALF * GROUP
BACK_VALUE = BACK_KEY + HALF * HD
VMEM_LIMIT = 40 * 1024 * 1024
BESIDE = 10**12
LOG2E = 1.4426950408889634
FACTOR = HD ** (-0.5)
VMEM = pl.BlockSpec(memory_space=pltpu.VMEM)
SMEM = pl.BlockSpec(memory_space=pltpu.SMEM)
ANY = pl.BlockSpec(memory_space=pl.ANY)

TASKS = {
    0: ((True, 2, (0, 2, 4)), (True, 3, (1, 3, 5))),
    1: ((False, 0, (0,)), (False, 1, (1,)), (False, 2, (2,)), (False, 3, (3,)), (True, 3, (4, 5))),
    2: ((False, 0, (0, 2)), (False, 1, (1, 3)), (False, 2, (4, 5))),
    3: ((False, 0, (0, 2, 4)), (False, 1, (1, 3, 5))),
}
HOST = {0: 3, 1: 2}
MOST = max(len(tasks) for tasks in TASKS.values())


def call(kernel, out_shape, in_specs, out_specs, scratch=(), flops=0, moved=0, grid=None):
    extra = {} if grid is None else {"grid": grid}
    return pl.pallas_call(
        kernel,
        out_shape=out_shape,
        in_specs=in_specs,
        out_specs=out_specs,
        scratch_shapes=list(scratch),
        cost_estimate=pl.CostEstimate(flops=flops, bytes_accessed=moved, transcendentals=0),
        compiler_params=pltpu.CompilerParams(vmem_limit_bytes=VMEM_LIMIT),
        **extra,
    )


def low(*shape):
    return jax.ShapeDtypeStruct(shape, jnp.bfloat16)


def full(*shape):
    return jax.ShapeDtypeStruct(shape, jnp.float32)


def near(*shape, dtype=jnp.bfloat16):
    return pltpu.VMEM(shape, dtype)


def far(*shape, dtype=jnp.bfloat16):
    return pltpu.HBM(shape, dtype)


def in_far(*arrays):
    return [pltpu.with_memory_space_constraint(array, pltpu.HBM) for array in arrays]


def wide_scratch(rows):
    return pltpu.VMEM((rows, HD), jnp.float32)


def pack_kernel(query_ref, grad_ref, key_ref, value_ref, out_ref, first_ref, second_ref, keys, values, wide, sems):
    half = HALF * GROUP
    copies = [
        pltpu.make_async_copy(key_ref, keys, sems.at[0]),
        pltpu.make_async_copy(value_ref, values, sems.at[1]),
        pltpu.make_async_copy(query_ref.at[:, half:], first_ref.at[:, :half], sems.at[2]),
        pltpu.make_async_copy(grad_ref.at[:, half:], second_ref.at[:, :half], sems.at[3]),
    ]
    for copy in copies:
        copy.start()
    for copy in copies[:2]:
        copy.wait()
    first_ref[:, half:] = keys[:, HALF * HD :]
    second_ref[:, half:] = values[:, HALF * HD :]
    for head in range(HEADS):
        lanes = slice(head * HD, (head + 1) * HD)
        wide[pl.ds(2 * head, ROWS, stride=TILE), :] = keys[:, lanes].astype(jnp.float32)
        wide[pl.ds(2 * head + 1, ROWS, stride=TILE), :] = values[:, lanes].astype(jnp.float32)
    out_ref[...] = wide[...].astype(jnp.bfloat16)
    for copy in copies[2:]:
        copy.wait()


def pack(queries, grad_output, keys, values):
    shapes = (near(ROWS * TILE, HD), near(ROWS, LENT), near(ROWS, LENT))
    scratch = [near(ROWS, WIDTH), near(ROWS, WIDTH), wide_scratch(ROWS * TILE), pltpu.SemaphoreType.DMA((4,))]
    return call(pack_kernel, shapes, [ANY] * 4, (VMEM,) * 3, scratch)(*in_far(queries, grad_output, keys, values))


def chain(parents_ref, level, seg):
    found = []
    current = seg
    for upper in range(level - 1, -1, -1):
        current = parents_ref[upper, current]
        found.insert(0, current)
    return found


def tile_at(upper, ancestor):
    return pl.ds(pl.multiple_of((upper * SEGS + ancestor) * TILE, TILE), TILE)


def rows_of(level, seg, first, count):
    return pl.ds((level * SEGS + seg) * PIECE + first, count)


def select_kernel(parents_ref, held_ref, out_ref, wide, picked):
    wide[...] = held_ref[...].astype(jnp.float32)

    def step(seg, carry):
        for upper, ancestor in enumerate(chain(parents_ref, 3, seg)):
            tile = wide[tile_at(upper, ancestor), :]
            picked[rows_of(3, seg, 4 * upper, 4), :] = tile[0:4]
            picked[rows_of(0, seg, 4 * upper, 4), :] = tile[4:8]
        first, second = [wide[tile_at(u, a), :] for u, a in enumerate(chain(parents_ref, 2, seg))]
        picked[rows_of(2, seg, 0, 4), :] = first[0:4]
        picked[rows_of(2, seg, 4, 4), :] = second[0:4]
        picked[rows_of(2, seg, 8, 2), :] = first[4:6]
        picked[rows_of(2, seg, 10, 2), :] = second[4:6]
        picked[rows_of(1, seg, 8, 2), :] = first[6:8]
        picked[rows_of(1, seg, 10, 2), :] = second[6:8]
        (only,) = chain(parents_ref, 1, seg)
        picked[rows_of(1, seg, 0, 8), :] = wide[tile_at(0, only), :]
        return carry

    lax.fori_loop(0, SEGS, step, 0, unroll=8)
    out_ref[...] = picked[...].astype(jnp.bfloat16)


def select(parents, held):
    scratch = [wide_scratch(DEVICES * TILE), wide_scratch(DEVICES * PIECE)]
    return call(select_kernel, near(DEVICES * PIECE, HD), [SMEM, VMEM], VMEM, scratch)(parents, held)


def sum_kernel(parents_ref, terms_ref, after_ref, out_ref, wide, *totals):
    wide[...] = terms_ref[...].astype(jnp.float32)
    for total in totals:
        total[...] = jnp.zeros_like(total)
    from_three, from_two, from_one = totals[:3], totals[3:5], totals[5]

    def rows(level, seg, first, count):
        return wide[rows_of(level, seg, first, count), :]

    def step(seg, carry):
        for upper, ancestor in enumerate(chain(parents_ref, 3, seg)):
            from_three[upper][tile_at(0, ancestor), :] += jnp.concatenate(
                [rows(3, seg, 4 * upper, 4), rows(0, seg, 4 * upper, 4)]
            )
        for upper, ancestor in enumerate(chain(parents_ref, 2, seg)):
            from_two[upper][tile_at(0, ancestor), :] += jnp.concatenate(
                [rows(2, seg, 4 * upper, 4), rows(2, seg, 8 + 2 * upper, 2), rows(1, seg, 8 + 2 * upper, 2)]
            )
        (only,) = chain(parents_ref, 1, seg)
        from_one[tile_at(0, only), :] += rows(1, seg, 0, 8)
        return carry

    lax.fori_loop(0, SEGS, step, 0, unroll=8)
    size = SEGS * TILE
    out_ref[0:size] = (from_three[0][...] + from_two[0][...] + from_one[...]).astype(jnp.bfloat16)
    out_ref[size : 2 * size] = (from_three[1][...] + from_two[1][...]).astype(jnp.bfloat16)
    out_ref[2 * size : 3 * size] = from_three[2][...].astype(jnp.bfloat16)
    out_ref[3 * size :] = jnp.zeros((size, HD), jnp.bfloat16)


def sum_terms(parents, terms, after):
    scratch = [wide_scratch(DEVICES * PIECE)] + [wide_scratch(SEGS * TILE)] * 6
    return call(sum_kernel, near(DEVICES * TILE, HD), [SMEM, VMEM, ANY], VMEM, scratch)(parents, terms, after)


def dot_last(left, right):
    return lax.dot_general(left, right, (((1,), (1,)), ((), ())), preferred_element_type=jnp.float32)


def dot(left, right):
    return jnp.dot(left, right, preferred_element_type=jnp.float32)


def block_mask(lengths):
    slots = lax.broadcasted_iota(jnp.int32, (ROWS, ROWS), 0)
    rows = lax.broadcasted_iota(jnp.int32, (ROWS, ROWS), 1)
    allowed = [slots < length for length in lengths]
    allowed[-1] = allowed[-1] & (slots <= rows)
    return jnp.concatenate([jnp.where(each, 0.0, -jnp.inf).astype(jnp.float32) for each in allowed])


def head_grad(keys, values, blocked, live_rows, query_at, grad_at, store):
    query = jnp.concatenate([query_at(i) for i in range(REPEAT)])
    grad = jnp.concatenate(
        [jnp.where(live_rows, grad_at(i), jnp.zeros((), jnp.bfloat16)) for i in range(REPEAT)]
    )
    scores = dot_last(keys, query) * (FACTOR * LOG2E) + jnp.concatenate([blocked] * REPEAT, axis=1)
    weights = jnp.exp2(scores - jnp.max(scores, axis=0, keepdims=True))
    probs = weights * (1.0 / jnp.sum(weights, axis=0, keepdims=True))
    grad_probs = dot_last(values, grad)
    correction = jnp.sum(probs * grad_probs, axis=0, keepdims=True)
    grad_scores = (probs * ((grad_probs - correction) * FACTOR)).astype(jnp.bfloat16)
    value_sum = dot(probs.astype(jnp.bfloat16), grad)
    key_sum = dot(grad_scores, query)
    turned = dot(keys.T, grad_scores).astype(jnp.bfloat16)
    for i in range(REPEAT):
        store(i, turned[:, i * ROWS : (i + 1) * ROWS].T)
    return key_sum, value_sum


def live(length):
    return lax.broadcasted_iota(jnp.int32, (ROWS, HD), 0) < length


def lanes_at(ref, start, width=HD):
    return ref.at[:, start : start + width]


def root_kernel(
    place_ref, lengths_ref, query_ref, grad_ref, key_ref, value_ref, guest_ref, after_ref,
    gquery_ref, gkey_ref, gvalue_ref,
    query, grad, keys, values, gquery, sems,
):
    @pl.when(place_ref[0] == 0)
    def _():
        pairs = ((query_ref, query), (grad_ref, grad), (key_ref, keys), (value_ref, values))
        copies = [pltpu.make_async_copy(*pair, sems.at[i]) for i, pair in enumerate(pairs)]
        for copy in copies:
            copy.start()
        for copy in copies:
            copy.wait()
        length = lengths_ref[0, place_ref[1]]
        blocked = block_mask([length])
        for head in range(HEADS):
            lanes = slice(head * HD, (head + 1) * HD)

            def store(i, block):
                lanes_at(gquery, head * GROUP + i * HD)[...] = block

            gkey_ref[:, lanes], gvalue_ref[:, lanes] = head_grad(
                keys[:, lanes],
                values[:, lanes],
                blocked,
                live(length),
                lambda i: lanes_at(query, head * GROUP + i * HD)[...],
                lambda i: lanes_at(grad, head * GROUP + i * HD)[...],
                store,
            )
        out = pltpu.make_async_copy(gquery, gquery_ref, sems.at[0])
        out.start()
        out.wait()


def root_grad(place, lengths, queries, grad_output, keys, values, guest, after):
    shapes = (
        far(ROWS, HEADS * GROUP), near(ROWS, WIDTH, dtype=jnp.float32), near(ROWS, WIDTH, dtype=jnp.float32)
    )
    specs = [SMEM, SMEM] + [ANY] * 6
    outs = (ANY, VMEM, VMEM)
    scratch = [
        near(ROWS, HEADS * GROUP), near(ROWS, HEADS * GROUP), near(ROWS, WIDTH), near(ROWS, WIDTH),
        near(ROWS, HEADS * GROUP), pltpu.SemaphoreType.DMA((4,)),
    ]
    return call(root_kernel, shapes, specs, outs, scratch, flops=BESIDE)(
        place, lengths, *in_far(queries, grad_output, keys, values), guest, after
    )


def attention_kernel(
    place_ref, parents_ref, lengths_ref,
    query_ref, grad_ref, key_ref, value_ref, first_ref, second_ref, held_ref, after_ref,
    gquery_ref, gkey_ref, gvalue_ref, back_ref, terms_ref,
    query, grad, keys, values, held, gquery, gkey, gvalue, back_own, wide, sums, in_sems, out_sems, held_sem,
):
    level_here = place_ref[0]
    seg = place_ref[1]

    def fetches(level, index):
        guest, head, _ = TASKS[level][index]
        if guest:
            wide_at, narrow_at = (head - HALF) * GROUP, HALF * GROUP + (head - HALF) * HD
            many = (first_ref, second_ref, first_ref, second_ref)
        else:
            wide_at, narrow_at = head * GROUP, head * HD
            many = (query_ref, grad_ref, key_ref, value_ref)
        sources = [lanes_at(ref, wide_at, GROUP) for ref in many[:2]] + [lanes_at(ref, narrow_at) for ref in many[2:]]
        return [
            pltpu.make_async_copy(source, target.at[index], in_sems.at[index, i])
            for i, (source, target) in enumerate(zip(sources, (query, grad, keys, values)))
        ]

    def result(level, index):
        guest, head, _ = TASKS[level][index]
        target = lanes_at(back_ref, (head - HALF) * GROUP, GROUP) if guest else lanes_at(gquery_ref, head * GROUP, GROUP)
        return pltpu.make_async_copy(gquery.at[index], target, out_sems.at[index])

    def at_level(level, body):
        pl.when(level_here == level)(body)

    def fetch_all(level):
        for index in range(len(TASKS[level])):
            for copy in fetches(level, index):
                copy.start()

    fetch_held = pltpu.make_async_copy(held_ref, held, held_sem)
    fetch_held.start()
    for level in range(LEVELS):
        at_level(level, lambda level=level: fetch_all(level))
    fetch_held.wait()
    wide[...] = held[...].astype(jnp.float32)

    def slot_rows(slot, part):
        return pl.ds(2 * slot + part, ROWS, stride=PIECE)

    def setting(level):
        lengths = [lengths_ref[u, a] for u, a in enumerate(chain(parents_ref, level, seg))]
        lengths.append(lengths_ref[level, seg])
        return block_mask(lengths), live(lengths[-1])

    def work(level, index, blocked, live_rows):
        slots = TASKS[level][index][2]
        key_list, value_list = [
            jnp.concatenate([wide[slot_rows(slot, part), :].astype(jnp.bfloat16) for slot in slots] + [mine[index]])
            for part, mine in enumerate((keys, values))
        ]

        def store(i, block):
            gquery[index, :, i * HD : (i + 1) * HD] = block

        key_sum, value_sum = head_grad(
            key_list,
            value_list,
            blocked,
            live_rows,
            lambda i: query[index, :, i * HD : (i + 1) * HD],
            lambda i: grad[index, :, i * HD : (i + 1) * HD],
            store,
        )
        for position, slot in enumerate(slots):
            block = slice(position * ROWS, (position + 1) * ROWS)
            sums[slot_rows(slot, 0), :] = key_sum[block]
            sums[slot_rows(slot, 1), :] = value_sum[block]
        gkey[index] = key_sum[len(slots) * ROWS :]
        gvalue[index] = value_sum[len(slots) * ROWS :]

    def work_on(level, indices, *settings):
        for index in indices:
            for copy in fetches(level, index):
                copy.wait()
        for index, (blocked, live_rows) in zip(indices, settings):
            work(level, index, blocked, live_rows)

    def send(level, indices):
        for index in indices:
            result(level, index).start()

    @pl.when((level_here == 3) | (level_here == 0))
    def _():
        work_on(3, (0, 1), *[setting(3)] * 2)
        at_level(3, lambda: send(3, (0, 1)))
        at_level(0, lambda: send(0, (0, 1)))

    @pl.when(level_here == 2)
    def _():
        both = setting(2)
        work_on(2, (0, 1), both, both)
        send(2, (0, 1))
        work_on(2, (2,), both)
        send(2, (2,))

    @pl.when(level_here == 1)
    def _():
        own, other = setting(1), setting(2)
        work_on(1, (4, 0), other, own)
        send(1, (4, 0))
        work_on(1, (1, 2, 3), own, own, own)
        send(1, (1, 2, 3))

    def hand_out(level):
        for index, (guest, head, _) in enumerate(TASKS[level]):
            if guest:
                place = head - HALF
                back_own[:, place * HD : (place + 1) * HD] = gkey[index].astype(jnp.bfloat16)
                back_own[:, (HALF + place) * HD : (HALF + place + 1) * HD] = gvalue[index].astype(jnp.bfloat16)
            else:
                gkey_ref[:, head * HD : (head + 1) * HD] = gkey[index]
                gvalue_ref[:, head * HD : (head + 1) * HD] = gvalue[index]
        own = pltpu.make_async_copy(back_own, lanes_at(back_ref, BACK_KEY, 2 * HALF * HD), in_sems.at[0, 0])
        if level in HOST:
            own.start()
            own.wait()
        for index in range(len(TASKS[level])):
            result(level, index).wait()

    terms_ref[...] = sums[...].astype(jnp.bfloat16)
    for level in range(LEVELS):
        at_level(level, lambda level=level: hand_out(level))


def attention(place, parents, lengths, queries, grad_output, keys, values, first, second, held, after):
    shapes = (
        far(ROWS, HEADS * GROUP), near(ROWS, WIDTH, dtype=jnp.float32), near(ROWS, WIDTH, dtype=jnp.float32),
        far(ROWS, BACK_VALUE + HALF * HD), near(ROWS * PIECE, HD),
    )
    specs = [SMEM] * 3 + [ANY] * 8
    outs = (ANY, VMEM, VMEM, ANY, VMEM)
    scratch = [
        near(MOST, ROWS, GROUP),
        near(MOST, ROWS, GROUP),
        near(MOST, ROWS, HD),
        near(MOST, ROWS, HD),
        near(ROWS * PIECE, HD),
        near(MOST, ROWS, GROUP),
        near(MOST, ROWS, HD, dtype=jnp.float32),
        near(MOST, ROWS, HD, dtype=jnp.float32),
        near(ROWS, 2 * HALF * HD),
        wide_scratch(ROWS * PIECE),
        wide_scratch(ROWS * PIECE),
        pltpu.SemaphoreType.DMA((MOST, 4)),
        pltpu.SemaphoreType.DMA((MOST,)),
        pltpu.SemaphoreType.DMA(()),
    ]
    return call(attention_kernel, shapes, specs, outs, scratch, flops=3 * 10**9, moved=10 * 2**20)(
        place, parents, lengths, *in_far(queries, grad_output, keys, values), first, second, held, after
    )


def token_kernel(after_ref, out_ref):
    out_ref[...] = jnp.zeros_like(out_ref)


def token(after):
    return call(token_kernel, full(8, HD), [ANY], VMEM, flops=BESIDE)(after)


def join_kernel(
    place_ref, root_ref, here_ref, back_ref, root_key_ref, here_key_ref, back_key_ref,
    root_value_ref, here_value_ref, back_value_ref, out_ref, key_ref, value_ref,
):
    level = place_ref[0]
    head = pl.program_id(0)
    away = ((level == 3) & (head >= HALF)) | ((level == 2) & (head == HEADS - 1))

    def take(source, key_source, value_source):
        out_ref[...] = source[...]
        key_ref[...] = key_source[...].astype(jnp.float32)
        value_ref[...] = value_source[...].astype(jnp.float32)

    pl.when(away)(lambda: take(back_ref, back_key_ref, back_value_ref))
    pl.when(level == 0)(lambda: take(root_ref, root_key_ref, root_value_ref))
    pl.when((level != 0) & jnp.logical_not(away))(lambda: take(here_ref, here_key_ref, here_value_ref))


def join(place, root, here, back):
    def spec(width, skipped, first):
        return pl.BlockSpec((ROWS, width), lambda h: (0, first // width + jnp.maximum(h - skipped, 0)))

    operands, specs = [place], [SMEM]
    for index, (width, first) in enumerate(((GROUP, 0), (HD, BACK_KEY), (HD, BACK_VALUE))):
        operands += [root[index], here[index], back]
        specs += [spec(width, 0, 0), spec(width, 0, 0), spec(width, HALF, first)]
    shapes = (low(ROWS, HEADS * GROUP), full(ROWS, WIDTH), full(ROWS, WIDTH))
    outs = (spec(GROUP, 0, 0), spec(HD, 0, 0), spec(HD, 0, 0))
    return call(join_kernel, shapes, specs, outs, grid=(HEADS,), moved=6 * 2**20)(*operands)


def finish_kernel(extra_ref, own_key_ref, own_value_ref, key_ref, value_ref, wide):
    wide[...] = extra_ref[...].astype(jnp.float32)
    for head in range(HEADS):
        lanes = slice(head * HD, (head + 1) * HD)
        for part, (own_ref, out_ref) in enumerate(((own_key_ref, key_ref), (own_value_ref, value_ref))):
            extra = wide[pl.ds(2 * head + part, ROWS, stride=TILE), :]
            out_ref[:, lanes] = (own_ref[:, lanes] + extra).astype(jnp.bfloat16)


def finish(extra, own_key, own_value):
    shapes = (low(ROWS, WIDTH), low(ROWS, WIDTH))
    return call(finish_kernel, shapes, [VMEM] * 3, (VMEM, VMEM), [wide_scratch(ROWS * TILE)])(
        extra, own_key, own_value
    )


def exchange(pieces, *tile):
    rows = pieces.shape[0]
    swapped = lax.all_to_all(pieces.reshape(DEVICES, *tile, HD), ("depth", "seg"), 0, 0, tiled=True)
    return swapped.reshape(rows, HD)


def per_device(queries, key_states, value_states, grad_output, parents, lengths):
    place = jnp.stack([lax.axis_index("depth"), lax.axis_index("seg")]).astype(jnp.int32)
    place, parents, lengths = in_far(place, parents, lengths)
    packed, *lent = pack(queries, grad_output, key_states, value_states)
    first, second = [lax.ppermute(each, "depth", [(host, here) for here, host in HOST.items()]) for each in lent]
    picked = select(parents, exchange(packed, TILE))
    arrived = exchange(picked, SLOTS // 2, 4)
    root = root_grad(place, lengths, queries, grad_output, key_states, value_states, first, picked)
    *here, back, terms = attention(
        place, parents, lengths, queries, grad_output, key_states, value_states, first, second, arrived, root[1]
    )
    back = lax.ppermute(back, "depth", list(HOST.items()))
    grad_q, own_k, own_v = join(place, root, here, back)
    extra = exchange(sum_terms(parents, exchange(terms, SLOTS // 2, 4), token(back)), TILE)
    grad_k, grad_v = finish(extra, own_k, own_v)
    return grad_q, grad_k, grad_v


def solution(mesh):
    placed = P(("depth", "seg"), "tp")
    return jax.shard_map(
        per_device,
        mesh=mesh,
        in_specs=(placed, placed, placed, placed, P(), P()),
        out_specs=(placed, placed, placed),
        check_vma=False,
    )
```

```python
import jax
import jax.numpy as jnp
from jax import lax
from jax.experimental import pallas as pl
from jax.experimental.pallas import tpu as pltpu
from jax.sharding import PartitionSpec as P

HD = 128
LEVELS = 4
SEGS = 32
ROWS = 128
HEADS = 4
REPEAT = 8
GROUP = REPEAT * HD
WIDTH = HEADS * HD
TILE = 2 * HEADS
UPPER = LEVELS - 1
DEVICES = LEVELS * SEGS
SLOTS = 6
PIECE = 2 * SLOTS
HALF = HEADS // 2
LENT = HALF * (GROUP + HD)
BACK_KEY = HALF * GROUP
BACK_VALUE = BACK_KEY + HALF * HD
VMEM_LIMIT = 32 * 1024 * 1024
BESIDE = 4 * 10**10
LOG2E = 1.4426950408889634
FACTOR = HD ** (-0.5)
VMEM = pl.BlockSpec(memory_space=pltpu.VMEM)
SMEM = pl.BlockSpec(memory_space=pltpu.SMEM)
ANY = pl.BlockSpec(memory_space=pl.ANY)

TASKS = {
    0: ((True, 2, (0, 2, 4)), (True, 3, (1, 3, 5))),
    1: ((False, 0, (0,)), (False, 1, (1,)), (False, 2, (2,)), (False, 3, (3,)), (True, 3, (4, 5))),
    2: ((False, 0, (0, 2)), (False, 1, (1, 3)), (False, 2, (4, 5))),
    3: ((False, 0, (0, 2, 4)), (False, 1, (1, 3, 5))),
}
HOST = {0: 3, 1: 2}
EARLY = {0: (0, 1), 1: (4, 0), 2: (0, 1), 3: (0, 1)}
LATE = {0: (), 1: (1, 2, 3), 2: (2,), 3: ()}
MOST = max(len(tasks) for tasks in TASKS.values())


def call(kernel, out_shape, in_specs, out_specs, scratch=(), flops=0, moved=0, grid=None):
    extra = {} if grid is None else {"grid": grid}
    return pl.pallas_call(
        kernel,
        out_shape=out_shape,
        in_specs=in_specs,
        out_specs=out_specs,
        scratch_shapes=list(scratch),
        cost_estimate=pl.CostEstimate(flops=flops, bytes_accessed=moved, transcendentals=0),
        compiler_params=pltpu.CompilerParams(vmem_limit_bytes=VMEM_LIMIT),
        **extra,
    )


def low(*shape):
    return jax.ShapeDtypeStruct(shape, jnp.bfloat16)


def full(*shape):
    return jax.ShapeDtypeStruct(shape, jnp.float32)


def near(*shape, dtype=jnp.bfloat16):
    return pltpu.VMEM(shape, dtype)


def far(*shape, dtype=jnp.bfloat16):
    return pltpu.HBM(shape, dtype)


def in_far(*arrays):
    return [pltpu.with_memory_space_constraint(array, pltpu.HBM) for array in arrays]


def in_near(*arrays):
    return [pltpu.with_memory_space_constraint(array, pltpu.VMEM) for array in arrays]


def wide_scratch(rows):
    return pltpu.VMEM((rows, HD), jnp.float32)


def pack_kernel(query_ref, grad_ref, key_ref, value_ref, out_ref, first_ref, second_ref, keys, values, wide, sems):
    half = HALF * GROUP
    copies = [
        pltpu.make_async_copy(key_ref, keys, sems.at[0]),
        pltpu.make_async_copy(value_ref, values, sems.at[1]),
        pltpu.make_async_copy(query_ref.at[:, half:], first_ref.at[:, :half], sems.at[2]),
        pltpu.make_async_copy(grad_ref.at[:, half:], second_ref.at[:, :half], sems.at[3]),
    ]
    for copy in copies:
        copy.start()
    for copy in copies[:2]:
        copy.wait()
    first_ref[:, half:] = keys[:, HALF * HD :]
    second_ref[:, half:] = values[:, HALF * HD :]
    for head in range(HEADS):
        lanes = slice(head * HD, (head + 1) * HD)
        wide[pl.ds(2 * head, ROWS, stride=TILE), :] = keys[:, lanes].astype(jnp.float32)
        wide[pl.ds(2 * head + 1, ROWS, stride=TILE), :] = values[:, lanes].astype(jnp.float32)
    out_ref[...] = wide[...].astype(jnp.bfloat16)
    for copy in copies[2:]:
        copy.wait()


def pack(queries, grad_output, keys, values):
    shapes = (near(ROWS * TILE, HD), near(ROWS, LENT), near(ROWS, LENT))
    scratch = [near(ROWS, WIDTH), near(ROWS, WIDTH), wide_scratch(ROWS * TILE), pltpu.SemaphoreType.DMA((4,))]
    return call(pack_kernel, shapes, [ANY] * 4, (VMEM,) * 3, scratch)(*in_far(queries, grad_output, keys, values))


def chain(parents_ref, level, seg):
    found = []
    current = seg
    for upper in range(level - 1, -1, -1):
        current = parents_ref[upper, current]
        found.insert(0, current)
    return found


def tile_at(upper, ancestor):
    return pl.ds(pl.multiple_of((upper * SEGS + ancestor) * TILE, TILE), TILE)


def rows_of(level, seg, first, count):
    return pl.ds((level * SEGS + seg) * PIECE + first, count)


def select_kernel(parents_ref, held_ref, out_ref, wide, picked):
    wide[...] = held_ref[...].astype(jnp.float32)

    def step(seg, carry):
        for upper, ancestor in enumerate(chain(parents_ref, 3, seg)):
            tile = wide[tile_at(upper, ancestor), :]
            picked[rows_of(3, seg, 4 * upper, 4), :] = tile[0:4]
            picked[rows_of(0, seg, 4 * upper, 4), :] = tile[4:8]
        first, second = [wide[tile_at(u, a), :] for u, a in enumerate(chain(parents_ref, 2, seg))]
        picked[rows_of(2, seg, 0, 4), :] = first[0:4]
        picked[rows_of(2, seg, 4, 4), :] = second[0:4]
        picked[rows_of(2, seg, 8, 2), :] = first[4:6]
        picked[rows_of(2, seg, 10, 2), :] = second[4:6]
        picked[rows_of(1, seg, 8, 2), :] = first[6:8]
        picked[rows_of(1, seg, 10, 2), :] = second[6:8]
        (only,) = chain(parents_ref, 1, seg)
        picked[rows_of(1, seg, 0, 8), :] = wide[tile_at(0, only), :]
        return carry

    lax.fori_loop(0, SEGS, step, 0, unroll=8)
    out_ref[...] = picked[...].astype(jnp.bfloat16)


def select(parents, held):
    scratch = [wide_scratch(DEVICES * TILE), wide_scratch(DEVICES * PIECE)]
    return call(select_kernel, near(DEVICES * PIECE, HD), [SMEM, VMEM], VMEM, scratch)(parents, held)


def sum_kernel(parents_ref, terms_ref, after_ref, out_ref, wide, *totals):
    wide[...] = terms_ref[...].astype(jnp.float32)
    for total in totals:
        total[...] = jnp.zeros_like(total)
    from_three, from_two, from_one = totals[:3], totals[3:5], totals[5]

    def rows(level, seg, first, count):
        return wide[rows_of(level, seg, first, count), :]

    def step(seg, carry):
        for upper, ancestor in enumerate(chain(parents_ref, 3, seg)):
            from_three[upper][tile_at(0, ancestor), :] += jnp.concatenate(
                [rows(3, seg, 4 * upper, 4), rows(0, seg, 4 * upper, 4)]
            )
        for upper, ancestor in enumerate(chain(parents_ref, 2, seg)):
            from_two[upper][tile_at(0, ancestor), :] += jnp.concatenate(
                [rows(2, seg, 4 * upper, 4), rows(2, seg, 8 + 2 * upper, 2), rows(1, seg, 8 + 2 * upper, 2)]
            )
        (only,) = chain(parents_ref, 1, seg)
        from_one[tile_at(0, only), :] += rows(1, seg, 0, 8)
        return carry

    lax.fori_loop(0, SEGS, step, 0, unroll=8)
    size = SEGS * TILE
    out_ref[0:size] = (from_three[0][...] + from_two[0][...] + from_one[...]).astype(jnp.bfloat16)
    out_ref[size : 2 * size] = (from_three[1][...] + from_two[1][...]).astype(jnp.bfloat16)
    out_ref[2 * size : 3 * size] = from_three[2][...].astype(jnp.bfloat16)
    out_ref[3 * size :] = jnp.zeros((size, HD), jnp.bfloat16)


def sum_terms(parents, terms, after):
    scratch = [wide_scratch(DEVICES * PIECE)] + [wide_scratch(SEGS * TILE)] * 6
    return call(sum_kernel, near(DEVICES * TILE, HD), [SMEM, VMEM, ANY], VMEM, scratch)(
        parents, *in_near(terms), after
    )


def dot_last(left, right):
    return lax.dot_general(left, right, (((1,), (1,)), ((), ())), preferred_element_type=jnp.float32)


def dot(left, right):
    return jnp.dot(left, right, preferred_element_type=jnp.float32)


def block_mask(lengths):
    slots = lax.broadcasted_iota(jnp.int32, (ROWS, ROWS), 0)
    rows = lax.broadcasted_iota(jnp.int32, (ROWS, ROWS), 1)
    allowed = [slots < length for length in lengths]
    allowed[-1] = allowed[-1] & (slots <= rows)
    return jnp.concatenate([jnp.where(each, 0.0, -jnp.inf).astype(jnp.float32) for each in allowed])


def head_grad(keys, values, blocked, live_rows, query_at, grad_at, store):
    query = jnp.concatenate([query_at(i) for i in range(REPEAT)])
    grad = jnp.concatenate(
        [jnp.where(live_rows, grad_at(i), jnp.zeros((), jnp.bfloat16)) for i in range(REPEAT)]
    )
    scores = dot_last(keys, query) * (FACTOR * LOG2E) + jnp.concatenate([blocked] * REPEAT, axis=1)
    weights = jnp.exp2(scores - jnp.max(scores, axis=0, keepdims=True))
    probs = weights * (1.0 / jnp.sum(weights, axis=0, keepdims=True))
    grad_probs = dot_last(values, grad)
    correction = jnp.sum(probs * grad_probs, axis=0, keepdims=True)
    grad_scores = (probs * ((grad_probs - correction) * FACTOR)).astype(jnp.bfloat16)
    value_sum = dot(probs.astype(jnp.bfloat16), grad)
    key_sum = dot(grad_scores, query)
    turned = dot(keys.T, grad_scores).astype(jnp.bfloat16)
    for i in range(REPEAT):
        store(i, turned[:, i * ROWS : (i + 1) * ROWS].T)
    return key_sum, value_sum


def live(length):
    return lax.broadcasted_iota(jnp.int32, (ROWS, HD), 0) < length


def lanes_at(ref, start, width=HD):
    return ref.at[:, start : start + width]


def root_kernel(
    place_ref, lengths_ref, query_ref, grad_ref, key_ref, value_ref, first_ref, second_ref, after_ref, picked_ref,
    gquery_ref, gkey_ref, gvalue_ref, query_tasks, grad_tasks, key_tasks, value_tasks,
    query, grad, keys, values, gquery, sems, task_sems,
):
    def fetches(level, index):
        guest, head, _ = TASKS[level][index]
        if guest:
            wide_at, narrow_at = (head - HALF) * GROUP, HALF * GROUP + (head - HALF) * HD
            many = (first_ref, second_ref, first_ref, second_ref)
        else:
            wide_at, narrow_at = head * GROUP, head * HD
            many = (query_ref, grad_ref, key_ref, value_ref)
        copies = [
            pltpu.make_async_copy(lanes_at(ref, narrow_at), target.at[index], task_sems.at[index, i])
            for i, (ref, target) in enumerate(zip(many[2:], (key_tasks, value_tasks)))
        ]
        if index in EARLY[level]:
            position = EARLY[level].index(index)
            copies += [
                pltpu.make_async_copy(lanes_at(ref, wide_at, GROUP), target.at[position], task_sems.at[index, 2 + i])
                for i, (ref, target) in enumerate(zip(many[:2], (query_tasks, grad_tasks)))
            ]
        return copies

    def gather(level):
        copies = [copy for index in range(len(TASKS[level])) for copy in fetches(level, index)]
        for copy in copies:
            copy.start()
        for copy in copies:
            copy.wait()

    for level in range(LEVELS):
        pl.when(place_ref[0] == level)(lambda level=level: gather(level))

    @pl.when(place_ref[0] == 0)
    def _():
        pairs = ((query_ref, query), (grad_ref, grad), (key_ref, keys), (value_ref, values))
        copies = [pltpu.make_async_copy(*pair, sems.at[i]) for i, pair in enumerate(pairs)]
        for copy in copies:
            copy.start()
        for copy in copies:
            copy.wait()
        length = lengths_ref[0, place_ref[1]]
        blocked = block_mask([length])
        for head in range(HEADS):
            lanes = slice(head * HD, (head + 1) * HD)

            def store(i, block):
                lanes_at(gquery, head * GROUP + i * HD)[...] = block

            gkey_ref[:, lanes], gvalue_ref[:, lanes] = head_grad(
                keys[:, lanes],
                values[:, lanes],
                blocked,
                live(length),
                lambda i: lanes_at(query, head * GROUP + i * HD)[...],
                lambda i: lanes_at(grad, head * GROUP + i * HD)[...],
                store,
            )
        out = pltpu.make_async_copy(gquery, gquery_ref, sems.at[0])
        out.start()
        out.wait()


def task_shapes():
    return near(2, ROWS, GROUP), near(2, ROWS, GROUP), near(MOST, ROWS, HD), near(MOST, ROWS, HD)


def root_grad(place, lengths, queries, grad_output, keys, values, first, second, *after):
    shapes = (
        far(ROWS, HEADS * GROUP), far(ROWS, WIDTH, dtype=jnp.float32), far(ROWS, WIDTH, dtype=jnp.float32),
    ) + task_shapes()
    specs = [SMEM, SMEM] + [ANY] * 8
    outs = (ANY,) + (VMEM,) * 6
    scratch = [
        near(ROWS, HEADS * GROUP), near(ROWS, HEADS * GROUP), near(ROWS, WIDTH), near(ROWS, WIDTH),
        near(ROWS, HEADS * GROUP), pltpu.SemaphoreType.DMA((4,)), pltpu.SemaphoreType.DMA((MOST, 4)),
    ]
    return call(root_kernel, shapes, specs, outs, scratch, flops=10**9, moved=6 * 2**20)(
        place, lengths, *in_far(queries, grad_output, keys, values), first, second, *after
    )


def attention_kernel(
    place_ref, parents_ref, lengths_ref, query_ref, grad_ref, query, grad, keys, values, held,
    gquery_ref, gkey_ref, gvalue_ref, back_ref, terms_ref,
    late_query, late_grad, gquery, gkey, gvalue, back_own, wide, sums, in_sems, out_sems, own_sem,
):
    level_here = place_ref[0]
    seg = place_ref[1]

    def result(level, index):
        guest, head, _ = TASKS[level][index]
        target = lanes_at(back_ref, (head - HALF) * GROUP, GROUP) if guest else lanes_at(gquery_ref, head * GROUP, GROUP)
        return pltpu.make_async_copy(gquery.at[index], target, out_sems.at[index])

    def at_level(level, body):
        pl.when(level_here == level)(body)

    def late(level, index):
        place, start = LATE[level].index(index), TASKS[level][index][1] * GROUP
        return [
            pltpu.make_async_copy(lanes_at(ref, start, GROUP), target.at[place], in_sems.at[place, i])
            for i, (ref, target) in enumerate(((query_ref, late_query), (grad_ref, late_grad)))
        ]

    def fetch_late(level):
        for index in LATE[level]:
            for copy in late(level, index):
                copy.start()

    for level in (1, 2):
        at_level(level, lambda level=level: fetch_late(level))
    wide[...] = held[...].astype(jnp.float32)

    def slot_rows(slot, part):
        return pl.ds(2 * slot + part, ROWS, stride=PIECE)

    def setting(level):
        lengths = [lengths_ref[u, a] for u, a in enumerate(chain(parents_ref, level, seg))]
        lengths.append(lengths_ref[level, seg])
        return block_mask(lengths), live(lengths[-1])

    def work(level, index, blocked, live_rows):
        slots = TASKS[level][index][2]
        key_list, value_list = [
            jnp.concatenate([wide[slot_rows(slot, part), :].astype(jnp.bfloat16) for slot in slots] + [mine[index]])
            for part, mine in enumerate((keys, values))
        ]

        if index in EARLY[level]:
            place, query_from, grad_from = EARLY[level].index(index), query, grad
        else:
            place, query_from, grad_from = LATE[level].index(index), late_query, late_grad

        def store(i, block):
            gquery[index, :, i * HD : (i + 1) * HD] = block

        key_sum, value_sum = head_grad(
            key_list,
            value_list,
            blocked,
            live_rows,
            lambda i: query_from[place, :, i * HD : (i + 1) * HD],
            lambda i: grad_from[place, :, i * HD : (i + 1) * HD],
            store,
        )
        for position, slot in enumerate(slots):
            block = slice(position * ROWS, (position + 1) * ROWS)
            sums[slot_rows(slot, 0), :] = key_sum[block]
            sums[slot_rows(slot, 1), :] = value_sum[block]
        gkey[index] = key_sum[len(slots) * ROWS :]
        gvalue[index] = value_sum[len(slots) * ROWS :]

    def work_on(level, indices, *settings):
        for index in indices:
            if index in LATE[level]:
                for copy in late(level, index):
                    copy.wait()
        for index, (blocked, live_rows) in zip(indices, settings):
            work(level, index, blocked, live_rows)

    def send(level, indices):
        for index in indices:
            result(level, index).start()

    @pl.when((level_here == 3) | (level_here == 0))
    def _():
        work_on(3, (0, 1), *[setting(3)] * 2)
        at_level(3, lambda: send(3, (0, 1)))
        at_level(0, lambda: send(0, (0, 1)))

    @pl.when(level_here == 2)
    def _():
        both = setting(2)
        work_on(2, (0, 1), both, both)
        send(2, (0, 1))
        work_on(2, (2,), both)
        send(2, (2,))

    @pl.when(level_here == 1)
    def _():
        own, other = setting(1), setting(2)
        work_on(1, (4, 0), other, own)
        send(1, (4, 0))
        work_on(1, (1, 2, 3), own, own, own)
        send(1, (1, 2, 3))

    def hand_out(level):
        for index, (guest, head, _) in enumerate(TASKS[level]):
            if guest:
                place = head - HALF
                back_own[:, place * HD : (place + 1) * HD] = gkey[index].astype(jnp.bfloat16)
                back_own[:, (HALF + place) * HD : (HALF + place + 1) * HD] = gvalue[index].astype(jnp.bfloat16)
            else:
                gkey_ref[:, head * HD : (head + 1) * HD] = gkey[index]
                gvalue_ref[:, head * HD : (head + 1) * HD] = gvalue[index]
        own = pltpu.make_async_copy(back_own, lanes_at(back_ref, BACK_KEY, 2 * HALF * HD), own_sem)
        if level in HOST:
            own.start()
            own.wait()
        for index in range(len(TASKS[level])):
            result(level, index).wait()

    terms_ref[...] = sums[...].astype(jnp.bfloat16)
    for level in range(LEVELS):
        at_level(level, lambda level=level: hand_out(level))


def attention(place, parents, lengths, queries, grad_output, tasks, held):
    shapes = (
        far(ROWS, HEADS * GROUP), far(ROWS, WIDTH, dtype=jnp.float32), far(ROWS, WIDTH, dtype=jnp.float32),
        far(ROWS, BACK_VALUE + HALF * HD), near(ROWS * PIECE, HD),
    )
    specs = [SMEM] * 3 + [ANY] * 2 + [VMEM] * 5
    outs = (ANY, VMEM, VMEM, ANY, VMEM)
    scratch = [
        near(MOST, ROWS, GROUP),
        near(MOST, ROWS, GROUP),
        near(MOST, ROWS, GROUP),
        near(MOST, ROWS, HD, dtype=jnp.float32),
        near(MOST, ROWS, HD, dtype=jnp.float32),
        near(ROWS, 2 * HALF * HD),
        wide_scratch(ROWS * PIECE),
        wide_scratch(ROWS * PIECE),
        pltpu.SemaphoreType.DMA((MOST, 2)),
        pltpu.SemaphoreType.DMA((MOST,)),
        pltpu.SemaphoreType.DMA(()),
    ]
    return call(attention_kernel, shapes, specs, outs, scratch, flops=3 * 10**9, moved=10 * 2**20)(
        place, parents, lengths, *in_far(queries, grad_output), *in_near(*tasks, held)
    )


def token_kernel(after_ref, out_ref):
    out_ref[...] = jnp.zeros_like(out_ref)


def token(after):
    return call(token_kernel, full(8, HD), [ANY], VMEM, flops=BESIDE)(after)


def join_kernel(
    place_ref, root_ref, here_ref, back_ref, root_key_ref, here_key_ref, back_key_ref,
    root_value_ref, here_value_ref, back_value_ref, out_ref, key_ref, value_ref,
):
    level = place_ref[0]
    head = pl.program_id(0)
    away = ((level == 3) & (head >= HALF)) | ((level == 2) & (head == HEADS - 1))

    def take(source, key_source, value_source):
        out_ref[...] = source[...]
        key_ref[...] = key_source[...].astype(jnp.float32)
        value_ref[...] = value_source[...].astype(jnp.float32)

    pl.when(away)(lambda: take(back_ref, back_key_ref, back_value_ref))
    pl.when(level == 0)(lambda: take(root_ref, root_key_ref, root_value_ref))
    pl.when((level != 0) & jnp.logical_not(away))(lambda: take(here_ref, here_key_ref, here_value_ref))


def join(place, root, here, back):
    def spec(width, skipped, first):
        return pl.BlockSpec((ROWS, width), lambda h: (0, first // width + jnp.maximum(h - skipped, 0)))

    root, here, operands, specs = in_far(*root), in_far(*here), [place], [SMEM]
    for index, (width, first) in enumerate(((GROUP, 0), (HD, BACK_KEY), (HD, BACK_VALUE))):
        operands += [root[index], here[index], back]
        specs += [spec(width, 0, 0), spec(width, 0, 0), spec(width, HALF, first)]
    shapes = (low(ROWS, HEADS * GROUP), full(ROWS, WIDTH), full(ROWS, WIDTH))
    outs = (spec(GROUP, 0, 0), spec(HD, 0, 0), spec(HD, 0, 0))
    return call(join_kernel, shapes, specs, outs, grid=(HEADS,), moved=6 * 2**20)(*operands)


def finish_kernel(extra_ref, own_key_ref, own_value_ref, key_ref, value_ref, wide):
    wide[...] = extra_ref[...].astype(jnp.float32)
    for head in range(HEADS):
        lanes = slice(head * HD, (head + 1) * HD)
        for part, (own_ref, out_ref) in enumerate(((own_key_ref, key_ref), (own_value_ref, value_ref))):
            extra = wide[pl.ds(2 * head + part, ROWS, stride=TILE), :]
            out_ref[:, lanes] = (own_ref[:, lanes] + extra).astype(jnp.bfloat16)


def finish(extra, own_key, own_value):
    shapes = (low(ROWS, WIDTH), low(ROWS, WIDTH))
    return call(finish_kernel, shapes, [VMEM] * 3, (VMEM, VMEM), [wide_scratch(ROWS * TILE)])(
        extra, own_key, own_value
    )


def exchange(pieces, *tile):
    rows = pieces.shape[0]
    swapped = lax.all_to_all(pieces.reshape(DEVICES, *tile, HD), ("depth", "seg"), 0, 0, tiled=True)
    return swapped.reshape(rows, HD)


def per_device(queries, key_states, value_states, grad_output, parents, lengths):
    place = jnp.stack([lax.axis_index("depth"), lax.axis_index("seg")]).astype(jnp.int32)
    place, parents, lengths = in_far(place, parents, lengths)
    packed, *lent = pack(queries, grad_output, key_states, value_states)
    first, second = [lax.ppermute(each, "depth", [(host, here) for here, host in HOST.items()]) for each in lent]
    picked = select(parents, exchange(packed, TILE))
    arrived = exchange(picked, SLOTS // 2, 4)
    *root, query_tasks, grad_tasks, key_tasks, value_tasks = root_grad(
        place, lengths, queries, grad_output, key_states, value_states, first, second, token(first), picked
    )
    tasks = (query_tasks, grad_tasks, key_tasks, value_tasks)
    *here, back, terms = attention(place, parents, lengths, queries, grad_output, tasks, arrived)
    back = lax.ppermute(back, "depth", list(HOST.items()))
    grad_q, own_k, own_v = join(place, root, here, back)
    extra = exchange(sum_terms(parents, exchange(terms, SLOTS // 2, 4), token(back)), TILE)
    grad_k, grad_v = finish(extra, own_k, own_v)
    return grad_q, grad_k, grad_v


def solution(mesh):
    placed = P(("depth", "seg"), "tp")
    return jax.shard_map(
        per_device,
        mesh=mesh,
        in_specs=(placed, placed, placed, placed, P(), P()),
        out_specs=(placed, placed, placed),
        check_vma=False,
    )
```

```python
import jax
import jax.numpy as jnp
from jax import lax
from jax.experimental import pallas as pl
from jax.experimental.pallas import tpu as pltpu
from jax.sharding import PartitionSpec as P

HD = 128
LEVELS = 4
SEGS = 32
ROWS = 128
HEADS = 4
REPEAT = 8
GROUP = REPEAT * HD
WIDTH = HEADS * HD
TILE = 2 * HEADS
UPPER = LEVELS - 1
DEVICES = LEVELS * SEGS
SLOTS = 6
PIECE = 2 * SLOTS
HALF = HEADS // 2
LENT = HALF * (GROUP + HD)
BACK_KEY = HALF * GROUP
BACK_VALUE = BACK_KEY + HALF * HD
VMEM_LIMIT = 32 * 1024 * 1024
BESIDE = 4 * 10**10
LOG2E = 1.4426950408889634
FACTOR = HD ** (-0.5)
VMEM = pl.BlockSpec(memory_space=pltpu.VMEM)
SMEM = pl.BlockSpec(memory_space=pltpu.SMEM)
ANY = pl.BlockSpec(memory_space=pl.ANY)

TASKS = {
    0: ((True, 2, (0, 2, 4)), (True, 3, (1, 3, 5))),
    1: ((False, 0, (0,)), (False, 1, (1,)), (False, 2, (2,)), (False, 3, (3,)), (True, 3, (4, 5))),
    2: ((False, 0, (0, 2)), (False, 1, (1, 3)), (False, 2, (4, 5))),
    3: ((False, 0, (0, 2, 4)), (False, 1, (1, 3, 5))),
}
HOST = {0: 3, 1: 2}
EARLY = {0: (0, 1), 1: (4, 0), 2: (0, 1), 3: (0, 1)}
LATE = {0: (), 1: (1, 2, 3), 2: (2,), 3: ()}
MOST = max(len(tasks) for tasks in TASKS.values())


def call(kernel, out_shape, in_specs, out_specs, scratch=(), flops=0, moved=0, grid=None):
    extra = {} if grid is None else {"grid": grid}
    return pl.pallas_call(
        kernel,
        out_shape=out_shape,
        in_specs=in_specs,
        out_specs=out_specs,
        scratch_shapes=list(scratch),
        cost_estimate=pl.CostEstimate(flops=flops, bytes_accessed=moved, transcendentals=0),
        compiler_params=pltpu.CompilerParams(vmem_limit_bytes=VMEM_LIMIT),
        **extra,
    )


def low(*shape):
    return jax.ShapeDtypeStruct(shape, jnp.bfloat16)


def full(*shape):
    return jax.ShapeDtypeStruct(shape, jnp.float32)


def near(*shape, dtype=jnp.bfloat16):
    return pltpu.VMEM(shape, dtype)


def far(*shape, dtype=jnp.bfloat16):
    return pltpu.HBM(shape, dtype)


def in_far(*arrays):
    return [pltpu.with_memory_space_constraint(array, pltpu.HBM) for array in arrays]


def in_near(*arrays):
    return [pltpu.with_memory_space_constraint(array, pltpu.VMEM) for array in arrays]


def wide_scratch(rows):
    return pltpu.VMEM((rows, HD), jnp.float32)


def pack_kernel(
    query_ref, grad_ref, key_ref, value_ref, out_ref, first_ref, second_ref, keys, values, packed, wide, sems
):
    half = HALF * GROUP
    copies = [
        pltpu.make_async_copy(key_ref, keys, sems.at[0]),
        pltpu.make_async_copy(value_ref, values, sems.at[1]),
        pltpu.make_async_copy(query_ref.at[:, half:], first_ref.at[:, :half], sems.at[2]),
        pltpu.make_async_copy(grad_ref.at[:, half:], second_ref.at[:, :half], sems.at[3]),
    ]
    for copy in copies:
        copy.start()
    for copy in copies[:2]:
        copy.wait()
    for head in range(HEADS):
        lanes = slice(head * HD, (head + 1) * HD)
        wide[pl.ds(2 * head, ROWS, stride=TILE), :] = keys[:, lanes].astype(jnp.float32)
        wide[pl.ds(2 * head + 1, ROWS, stride=TILE), :] = values[:, lanes].astype(jnp.float32)
    packed[...] = wide[...].astype(jnp.bfloat16)
    out = pltpu.make_async_copy(packed, out_ref, sems.at[0])
    out.start()
    first_ref[:, half:] = keys[:, HALF * HD :]
    second_ref[:, half:] = values[:, HALF * HD :]
    for copy in copies[2:] + [out]:
        copy.wait()


def pack(queries, grad_output, keys, values):
    shapes = (far(ROWS * TILE, HD), near(ROWS, LENT), near(ROWS, LENT))
    scratch = [near(ROWS, WIDTH), near(ROWS, WIDTH), near(ROWS * TILE, HD), wide_scratch(ROWS * TILE)]
    scratch.append(pltpu.SemaphoreType.DMA((4,)))
    return call(pack_kernel, shapes, [ANY] * 4, (ANY, VMEM, VMEM), scratch)(*in_far(queries, grad_output, keys, values))


def chain(parents_ref, level, seg):
    found = []
    current = seg
    for upper in range(level - 1, -1, -1):
        current = parents_ref[upper, current]
        found.insert(0, current)
    return found


def tile_at(upper, ancestor):
    return pl.ds(pl.multiple_of((upper * SEGS + ancestor) * TILE, TILE), TILE)


def rows_of(level, seg, first, count):
    return pl.ds((level * SEGS + seg) * PIECE + first, count)


def select_kernel(parents_ref, held_ref, out_ref, wide, picked):
    wide[...] = held_ref[...].astype(jnp.float32)

    def step(seg, carry):
        for upper, ancestor in enumerate(chain(parents_ref, 3, seg)):
            tile = wide[tile_at(upper, ancestor), :]
            picked[rows_of(3, seg, 4 * upper, 4), :] = tile[0:4]
            picked[rows_of(0, seg, 4 * upper, 4), :] = tile[4:8]
        first, second = [wide[tile_at(u, a), :] for u, a in enumerate(chain(parents_ref, 2, seg))]
        picked[rows_of(2, seg, 0, 4), :] = first[0:4]
        picked[rows_of(2, seg, 4, 4), :] = second[0:4]
        picked[rows_of(2, seg, 8, 2), :] = first[4:6]
        picked[rows_of(2, seg, 10, 2), :] = second[4:6]
        picked[rows_of(1, seg, 8, 2), :] = first[6:8]
        picked[rows_of(1, seg, 10, 2), :] = second[6:8]
        (only,) = chain(parents_ref, 1, seg)
        picked[rows_of(1, seg, 0, 8), :] = wide[tile_at(0, only), :]
        return carry

    lax.fori_loop(0, SEGS, step, 0, unroll=True)
    out_ref[...] = picked[...].astype(jnp.bfloat16)


def select(parents, held):
    scratch = [wide_scratch(DEVICES * TILE), wide_scratch(DEVICES * PIECE)]
    return call(select_kernel, near(DEVICES * PIECE, HD), [SMEM, VMEM], VMEM, scratch)(parents, held)


def sum_kernel(parents_ref, terms_ref, after_ref, out_ref, wide, *totals):
    wide[...] = terms_ref[...].astype(jnp.float32)
    for total in totals:
        total[...] = jnp.zeros_like(total)
    from_three, from_two, from_one = totals[:3], totals[3:5], totals[5]

    def rows(level, seg, first, count):
        return wide[rows_of(level, seg, first, count), :]

    def step(seg, carry):
        for upper, ancestor in enumerate(chain(parents_ref, 3, seg)):
            from_three[upper][tile_at(0, ancestor), :] += jnp.concatenate(
                [rows(3, seg, 4 * upper, 4), rows(0, seg, 4 * upper, 4)]
            )
        for upper, ancestor in enumerate(chain(parents_ref, 2, seg)):
            from_two[upper][tile_at(0, ancestor), :] += jnp.concatenate(
                [rows(2, seg, 4 * upper, 4), rows(2, seg, 8 + 2 * upper, 2), rows(1, seg, 8 + 2 * upper, 2)]
            )
        (only,) = chain(parents_ref, 1, seg)
        from_one[tile_at(0, only), :] += rows(1, seg, 0, 8)
        return carry

    lax.fori_loop(0, SEGS, step, 0, unroll=True)
    size = SEGS * TILE
    out_ref[0:size] = (from_three[0][...] + from_two[0][...] + from_one[...]).astype(jnp.bfloat16)
    out_ref[size : 2 * size] = (from_three[1][...] + from_two[1][...]).astype(jnp.bfloat16)
    out_ref[2 * size : 3 * size] = from_three[2][...].astype(jnp.bfloat16)
    out_ref[3 * size :] = jnp.zeros((size, HD), jnp.bfloat16)


def sum_terms(parents, terms, after):
    scratch = [wide_scratch(DEVICES * PIECE)] + [wide_scratch(SEGS * TILE)] * 6
    return call(sum_kernel, near(DEVICES * TILE, HD), [SMEM, VMEM, ANY], VMEM, scratch)(
        parents, *in_near(terms), after
    )


def dot_last(left, right):
    return lax.dot_general(left, right, (((1,), (1,)), ((), ())), preferred_element_type=jnp.float32)


def dot(left, right):
    return jnp.dot(left, right, preferred_element_type=jnp.float32)


def block_mask(lengths):
    slots = lax.broadcasted_iota(jnp.int32, (ROWS, ROWS), 0)
    rows = lax.broadcasted_iota(jnp.int32, (ROWS, ROWS), 1)
    allowed = [slots < length for length in lengths]
    allowed[-1] = allowed[-1] & (slots <= rows)
    return jnp.concatenate([jnp.where(each, 0.0, -jnp.inf).astype(jnp.float32) for each in allowed])


def head_grad(keys, values, blocked, live_rows, query_at, grad_at, store):
    query = jnp.concatenate([query_at(i) for i in range(REPEAT)])
    grad = jnp.concatenate(
        [jnp.where(live_rows, grad_at(i), jnp.zeros((), jnp.bfloat16)) for i in range(REPEAT)]
    )
    scores = dot_last(keys, query) * (FACTOR * LOG2E) + jnp.concatenate([blocked] * REPEAT, axis=1)
    weights = jnp.exp2(scores - jnp.max(scores, axis=0, keepdims=True))
    probs = weights * (1.0 / jnp.sum(weights, axis=0, keepdims=True))
    grad_probs = dot_last(values, grad)
    correction = jnp.sum(probs * grad_probs, axis=0, keepdims=True)
    grad_scores = (probs * ((grad_probs - correction) * FACTOR)).astype(jnp.bfloat16)
    value_sum = dot(probs.astype(jnp.bfloat16), grad)
    key_sum = dot(grad_scores, query)
    turned = dot(keys.T, grad_scores).astype(jnp.bfloat16)
    for i in range(REPEAT):
        store(i, turned[:, i * ROWS : (i + 1) * ROWS].T)
    return key_sum, value_sum


def live(length):
    return lax.broadcasted_iota(jnp.int32, (ROWS, HD), 0) < length


def lanes_at(ref, start, width=HD):
    return ref.at[:, start : start + width]


def root_kernel(
    place_ref, lengths_ref, query_ref, grad_ref, key_ref, value_ref, first_ref, second_ref, after_ref, picked_ref,
    gquery_ref, gkey_ref, gvalue_ref, query_tasks, grad_tasks, key_tasks, value_tasks,
    query, grad, keys, values, gquery, sems, task_sems,
):
    def fetches(level, index):
        guest, head, _ = TASKS[level][index]
        if guest:
            wide_at, narrow_at = (head - HALF) * GROUP, HALF * GROUP + (head - HALF) * HD
            many = (first_ref, second_ref, first_ref, second_ref)
        else:
            wide_at, narrow_at = head * GROUP, head * HD
            many = (query_ref, grad_ref, key_ref, value_ref)
        copies = [
            pltpu.make_async_copy(lanes_at(ref, narrow_at), target.at[index], task_sems.at[index, i])
            for i, (ref, target) in enumerate(zip(many[2:], (key_tasks, value_tasks)))
        ]
        if index in EARLY[level]:
            position = EARLY[level].index(index)
            copies += [
                pltpu.make_async_copy(lanes_at(ref, wide_at, GROUP), target.at[position], task_sems.at[index, 2 + i])
                for i, (ref, target) in enumerate(zip(many[:2], (query_tasks, grad_tasks)))
            ]
        return copies

    def gather(level):
        copies = [copy for index in range(len(TASKS[level])) for copy in fetches(level, index)]
        for copy in copies:
            copy.start()
        for copy in copies:
            copy.wait()

    for level in range(LEVELS):
        pl.when(place_ref[0] == level)(lambda level=level: gather(level))

    @pl.when(place_ref[0] == 0)
    def _():
        pairs = ((query_ref, query), (grad_ref, grad), (key_ref, keys), (value_ref, values))
        copies = [pltpu.make_async_copy(*pair, sems.at[i]) for i, pair in enumerate(pairs)]
        for copy in copies:
            copy.start()
        for copy in copies:
            copy.wait()
        length = lengths_ref[0, place_ref[1]]
        blocked = block_mask([length])
        for head in range(HEADS):
            lanes = slice(head * HD, (head + 1) * HD)

            def store(i, block):
                lanes_at(gquery, head * GROUP + i * HD)[...] = block

            gkey_ref[:, lanes], gvalue_ref[:, lanes] = head_grad(
                keys[:, lanes],
                values[:, lanes],
                blocked,
                live(length),
                lambda i: lanes_at(query, head * GROUP + i * HD)[...],
                lambda i: lanes_at(grad, head * GROUP + i * HD)[...],
                store,
            )
        out = pltpu.make_async_copy(gquery, gquery_ref, sems.at[0])
        out.start()
        out.wait()


def task_shapes():
    return near(2, ROWS, GROUP), near(2, ROWS, GROUP), near(MOST, ROWS, HD), near(MOST, ROWS, HD)


def root_grad(place, lengths, queries, grad_output, keys, values, first, second, *after):
    shapes = (
        far(ROWS, HEADS * GROUP), far(ROWS, WIDTH, dtype=jnp.float32), far(ROWS, WIDTH, dtype=jnp.float32),
    ) + task_shapes()
    specs = [SMEM, SMEM] + [ANY] * 8
    outs = (ANY,) + (VMEM,) * 6
    scratch = [
        near(ROWS, HEADS * GROUP), near(ROWS, HEADS * GROUP), near(ROWS, WIDTH), near(ROWS, WIDTH),
        near(ROWS, HEADS * GROUP), pltpu.SemaphoreType.DMA((4,)), pltpu.SemaphoreType.DMA((MOST, 4)),
    ]
    return call(root_kernel, shapes, specs, outs, scratch, flops=10**9, moved=6 * 2**20)(
        place, lengths, *in_far(queries, grad_output, keys, values), first, second, *after
    )


def attention_kernel(
    place_ref, parents_ref, lengths_ref, query_ref, grad_ref, query, grad, keys, values, held,
    gquery_ref, gkey_ref, gvalue_ref, back_ref, terms_ref,
    late_query, late_grad, gquery, gkey, gvalue, back_own, wide, sums, terms_low, in_sems, out_sems, own_sems,
):
    level_here = place_ref[0]
    seg = place_ref[1]

    def result(level, index):
        guest, head, _ = TASKS[level][index]
        target = lanes_at(back_ref, (head - HALF) * GROUP, GROUP) if guest else lanes_at(gquery_ref, head * GROUP, GROUP)
        return pltpu.make_async_copy(gquery.at[index], target, out_sems.at[index])

    def at_level(level, body):
        pl.when(level_here == level)(body)

    def late(level, index):
        place, start = LATE[level].index(index), TASKS[level][index][1] * GROUP
        return [
            pltpu.make_async_copy(lanes_at(ref, start, GROUP), target.at[place], in_sems.at[place, i])
            for i, (ref, target) in enumerate(((query_ref, late_query), (grad_ref, late_grad)))
        ]

    def fetch_late(level):
        for index in LATE[level]:
            for copy in late(level, index):
                copy.start()

    for level in (1, 2):
        at_level(level, lambda level=level: fetch_late(level))
    wide[...] = held[...].astype(jnp.float32)

    def slot_rows(slot, part):
        return pl.ds(2 * slot + part, ROWS, stride=PIECE)

    def setting(level):
        lengths = [lengths_ref[u, a] for u, a in enumerate(chain(parents_ref, level, seg))]
        lengths.append(lengths_ref[level, seg])
        return block_mask(lengths), live(lengths[-1])

    def work(level, index, blocked, live_rows):
        slots = TASKS[level][index][2]
        key_list, value_list = [
            jnp.concatenate([wide[slot_rows(slot, part), :].astype(jnp.bfloat16) for slot in slots] + [mine[index]])
            for part, mine in enumerate((keys, values))
        ]

        if index in EARLY[level]:
            place, query_from, grad_from = EARLY[level].index(index), query, grad
        else:
            place, query_from, grad_from = LATE[level].index(index), late_query, late_grad

        def store(i, block):
            gquery[index, :, i * HD : (i + 1) * HD] = block

        key_sum, value_sum = head_grad(
            key_list,
            value_list,
            blocked,
            live_rows,
            lambda i: query_from[place, :, i * HD : (i + 1) * HD],
            lambda i: grad_from[place, :, i * HD : (i + 1) * HD],
            store,
        )
        for position, slot in enumerate(slots):
            block = slice(position * ROWS, (position + 1) * ROWS)
            sums[slot_rows(slot, 0), :] = key_sum[block]
            sums[slot_rows(slot, 1), :] = value_sum[block]
        gkey[index] = key_sum[len(slots) * ROWS :]
        gvalue[index] = value_sum[len(slots) * ROWS :]

    def work_on(level, indices, *settings):
        for index in indices:
            if index in LATE[level]:
                for copy in late(level, index):
                    copy.wait()
        for index, (blocked, live_rows) in zip(indices, settings):
            work(level, index, blocked, live_rows)

    def send(level, indices):
        for index in indices:
            result(level, index).start()

    @pl.when((level_here == 3) | (level_here == 0))
    def _():
        work_on(3, (0, 1), *[setting(3)] * 2)
        at_level(3, lambda: send(3, (0, 1)))
        at_level(0, lambda: send(0, (0, 1)))

    @pl.when(level_here == 2)
    def _():
        both = setting(2)
        work_on(2, (0, 1), both, both)
        send(2, (0, 1))
        work_on(2, (2,), both)
        send(2, (2,))

    @pl.when(level_here == 1)
    def _():
        own, other = setting(1), setting(2)
        work_on(1, (4, 0), other, own)
        send(1, (4, 0))
        work_on(1, (1, 2, 3), own, own, own)
        send(1, (1, 2, 3))

    terms_low[...] = sums[...].astype(jnp.bfloat16)
    terms_out = pltpu.make_async_copy(terms_low, terms_ref, own_sems.at[0])
    terms_out.start()

    def hand_out(level):
        copies = []
        for index, (guest, head, _) in enumerate(TASKS[level]):
            if guest:
                place = head - HALF
                back_own[:, place * HD : (place + 1) * HD] = gkey[index].astype(jnp.bfloat16)
                back_own[:, (HALF + place) * HD : (HALF + place + 1) * HD] = gvalue[index].astype(jnp.bfloat16)
            else:
                for i, (source, target) in enumerate(((gkey, gkey_ref), (gvalue, gvalue_ref))):
                    copies.append(
                        pltpu.make_async_copy(source.at[index], lanes_at(target, head * HD), in_sems.at[index, i])
                    )
        if level in HOST:
            copies.append(pltpu.make_async_copy(back_own, lanes_at(back_ref, BACK_KEY, 2 * HALF * HD), own_sems.at[1]))
        for copy in copies:
            copy.start()
        for copy in copies + [result(level, index) for index in range(len(TASKS[level]))]:
            copy.wait()

    for level in range(LEVELS):
        at_level(level, lambda level=level: hand_out(level))
    terms_out.wait()


def attention(place, parents, lengths, queries, grad_output, tasks, held):
    shapes = (
        far(ROWS, HEADS * GROUP), far(ROWS, WIDTH, dtype=jnp.float32), far(ROWS, WIDTH, dtype=jnp.float32),
        far(ROWS, BACK_VALUE + HALF * HD), far(ROWS * PIECE, HD),
    )
    specs = [SMEM] * 3 + [ANY] * 2 + [VMEM] * 5
    outs = (ANY,) * 5
    scratch = [
        near(MOST, ROWS, GROUP),
        near(MOST, ROWS, GROUP),
        near(MOST, ROWS, GROUP),
        near(MOST, ROWS, HD, dtype=jnp.float32),
        near(MOST, ROWS, HD, dtype=jnp.float32),
        near(ROWS, 2 * HALF * HD),
        wide_scratch(ROWS * PIECE),
        wide_scratch(ROWS * PIECE),
        near(ROWS * PIECE, HD),
        pltpu.SemaphoreType.DMA((MOST, 2)),
        pltpu.SemaphoreType.DMA((MOST,)),
        pltpu.SemaphoreType.DMA((2,)),
    ]
    return call(attention_kernel, shapes, specs, outs, scratch, flops=3 * 10**9, moved=10 * 2**20)(
        place, parents, lengths, *in_far(queries, grad_output), *in_near(*tasks, held)
    )


def token_kernel(after_ref, out_ref):
    out_ref[...] = jnp.zeros_like(out_ref)


def token(after):
    return call(token_kernel, full(8, HD), [ANY], VMEM, flops=BESIDE)(after)


def join_kernel(
    place_ref, root_ref, here_ref, back_ref, root_key_ref, here_key_ref, back_key_ref,
    root_value_ref, here_value_ref, back_value_ref, out_ref, key_ref, value_ref,
):
    level = place_ref[0]
    head = pl.program_id(0)
    away = ((level == 3) & (head >= HALF)) | ((level == 2) & (head == HEADS - 1))

    def take(source, key_source, value_source):
        out_ref[...] = source[...]
        key_ref[...] = key_source[...].astype(jnp.float32)
        value_ref[...] = value_source[...].astype(jnp.float32)

    pl.when(away)(lambda: take(back_ref, back_key_ref, back_value_ref))
    pl.when(level == 0)(lambda: take(root_ref, root_key_ref, root_value_ref))
    pl.when((level != 0) & jnp.logical_not(away))(lambda: take(here_ref, here_key_ref, here_value_ref))


def join(place, root, here, back):
    def spec(width, skipped, first):
        return pl.BlockSpec((ROWS, width), lambda h: (0, first // width + jnp.maximum(h - skipped, 0)))

    root, here, operands, specs = in_far(*root), in_far(*here), [place], [SMEM]
    for index, (width, first) in enumerate(((GROUP, 0), (HD, BACK_KEY), (HD, BACK_VALUE))):
        operands += [root[index], here[index], back]
        specs += [spec(width, 0, 0), spec(width, 0, 0), spec(width, HALF, first)]
    shapes = (low(ROWS, HEADS * GROUP), full(ROWS, WIDTH), full(ROWS, WIDTH))
    outs = (spec(GROUP, 0, 0), spec(HD, 0, 0), spec(HD, 0, 0))
    return call(join_kernel, shapes, specs, outs, grid=(HEADS,), moved=6 * 2**20)(*operands)


def finish_kernel(extra_ref, own_key_ref, own_value_ref, key_ref, value_ref, wide):
    wide[...] = extra_ref[...].astype(jnp.float32)
    for head in range(HEADS):
        lanes = slice(head * HD, (head + 1) * HD)
        for part, (own_ref, out_ref) in enumerate(((own_key_ref, key_ref), (own_value_ref, value_ref))):
            extra = wide[pl.ds(2 * head + part, ROWS, stride=TILE), :]
            out_ref[:, lanes] = (own_ref[:, lanes] + extra).astype(jnp.bfloat16)


def finish(extra, own_key, own_value):
    shapes = (low(ROWS, WIDTH), low(ROWS, WIDTH))
    return call(finish_kernel, shapes, [VMEM] * 3, (VMEM, VMEM), [wide_scratch(ROWS * TILE)])(
        extra, own_key, own_value
    )


def exchange(pieces, *tile):
    rows = pieces.shape[0]
    swapped = lax.all_to_all(pieces.reshape(DEVICES, *tile, HD), ("depth", "seg"), 0, 0, tiled=True)
    return swapped.reshape(rows, HD)


def per_device(queries, key_states, value_states, grad_output, parents, lengths):
    place = jnp.stack([lax.axis_index("depth"), lax.axis_index("seg")]).astype(jnp.int32)
    place, parents, lengths = [pltpu.with_memory_space_constraint(x, pltpu.SMEM) for x in (place, parents, lengths)]
    packed, *lent = pack(queries, grad_output, key_states, value_states)
    first, second = [lax.ppermute(each, "depth", [(host, here) for here, host in HOST.items()]) for each in lent]
    picked = select(parents, exchange(packed, TILE))
    arrived = exchange(picked, SLOTS // 2, 4)
    *root, query_tasks, grad_tasks, key_tasks, value_tasks = root_grad(
        place, lengths, queries, grad_output, key_states, value_states, first, second, token(first), picked
    )
    tasks = (query_tasks, grad_tasks, key_tasks, value_tasks)
    *here, back, terms = attention(place, parents, lengths, queries, grad_output, tasks, arrived)
    back = lax.ppermute(back, "depth", list(HOST.items()))
    grad_q, own_k, own_v = join(place, root, here, back)
    extra = exchange(sum_terms(parents, exchange(terms, SLOTS // 2, 4), token(back)), TILE)
    grad_k, grad_v = finish(extra, own_k, own_v)
    return grad_q, grad_k, grad_v


def solution(mesh):
    placed = P(("depth", "seg"), "tp")
    return jax.shard_map(
        per_device,
        mesh=mesh,
        in_specs=(placed, placed, placed, placed, P(), P()),
        out_specs=(placed, placed, placed),
        check_vma=False,
    )
```

```python
import jax
import jax.numpy as jnp
from jax import lax
from jax.experimental import pallas as pl
from jax.experimental.pallas import tpu as pltpu
from jax.sharding import PartitionSpec as P

HD = 128
LEVELS = 4
SEGS = 32
ROWS = 128
HEADS = 4
REPEAT = 8
GROUP = REPEAT * HD
WIDTH = HEADS * HD
TILE = 2 * HEADS
UPPER = LEVELS - 1
DEVICES = LEVELS * SEGS
SLOTS = 6
PIECE = 2 * SLOTS
HALF = HEADS // 2
LENT = HALF * (GROUP + HD)
BACK_KEY = HALF * GROUP
BACK_VALUE = BACK_KEY + HALF * HD
VMEM_LIMIT = 32 * 1024 * 1024
BESIDE = 4 * 10**10
LOG2E = 1.4426950408889634
FACTOR = HD ** (-0.5)
VMEM = pl.BlockSpec(memory_space=pltpu.VMEM)
SMEM = pl.BlockSpec(memory_space=pltpu.SMEM)
ANY = pl.BlockSpec(memory_space=pl.ANY)

TASKS = {
    0: ((True, 2, (0, 2, 4)), (True, 3, (1, 3, 5))),
    1: ((False, 0, (0,)), (False, 1, (1,)), (False, 2, (2,)), (False, 3, (3,)), (True, 3, (4, 5))),
    2: ((False, 0, (0, 2)), (False, 1, (1, 3)), (False, 2, (4, 5))),
    3: ((False, 0, (0, 2, 4)), (False, 1, (1, 3, 5))),
}
HOST = {0: 3, 1: 2}
EARLY = {0: (0, 1), 1: (4, 0), 2: (0, 1), 3: (0, 1)}
LATE = {0: (), 1: (1, 2, 3), 2: (2,), 3: ()}
MOST = max(len(tasks) for tasks in TASKS.values())


def call(kernel, out_shape, in_specs, out_specs, scratch=(), flops=0, moved=0, grid=None):
    extra = {} if grid is None else {"grid": grid}
    return pl.pallas_call(
        kernel,
        out_shape=out_shape,
        in_specs=in_specs,
        out_specs=out_specs,
        scratch_shapes=list(scratch),
        cost_estimate=pl.CostEstimate(flops=flops, bytes_accessed=moved, transcendentals=0),
        compiler_params=pltpu.CompilerParams(vmem_limit_bytes=VMEM_LIMIT),
        **extra,
    )


def low(*shape):
    return jax.ShapeDtypeStruct(shape, jnp.bfloat16)


def full(*shape):
    return jax.ShapeDtypeStruct(shape, jnp.float32)


def near(*shape, dtype=jnp.bfloat16):
    return pltpu.VMEM(shape, dtype)


def far(*shape, dtype=jnp.bfloat16):
    return pltpu.HBM(shape, dtype)


def in_far(*arrays):
    return [pltpu.with_memory_space_constraint(array, pltpu.HBM) for array in arrays]


def in_near(*arrays):
    return [pltpu.with_memory_space_constraint(array, pltpu.VMEM) for array in arrays]


def wide_scratch(rows):
    return pltpu.VMEM((rows + 16, HD), jnp.float32)


def pack_kernel(
    query_ref, grad_ref, key_ref, value_ref, out_ref, first_ref, second_ref, keys, values, packed, wide, sems
):
    half = HALF * GROUP
    copies = [
        pltpu.make_async_copy(key_ref, keys, sems.at[0]),
        pltpu.make_async_copy(value_ref, values, sems.at[1]),
        pltpu.make_async_copy(query_ref.at[:, half:], first_ref.at[:, :half], sems.at[2]),
        pltpu.make_async_copy(grad_ref.at[:, half:], second_ref.at[:, :half], sems.at[3]),
    ]
    for copy in copies:
        copy.start()
    for copy in copies[:2]:
        copy.wait()
    for head in range(HEADS):
        lanes = slice(head * HD, (head + 1) * HD)
        wide[pl.ds(2 * head, ROWS, stride=TILE), :] = keys[:, lanes].astype(jnp.float32)
        wide[pl.ds(2 * head + 1, ROWS, stride=TILE), :] = values[:, lanes].astype(jnp.float32)
    packed[...] = wide[0 : ROWS * TILE].astype(jnp.bfloat16)
    out = pltpu.make_async_copy(packed, out_ref, sems.at[0])
    out.start()
    first_ref[:, half:] = keys[:, HALF * HD :]
    second_ref[:, half:] = values[:, HALF * HD :]
    for copy in copies[2:] + [out]:
        copy.wait()


def pack(queries, grad_output, keys, values):
    shapes = (far(ROWS * TILE, HD), near(ROWS, LENT), near(ROWS, LENT))
    scratch = [near(ROWS, WIDTH), near(ROWS, WIDTH), near(ROWS * TILE, HD), wide_scratch(ROWS * TILE)]
    scratch.append(pltpu.SemaphoreType.DMA((4,)))
    return call(pack_kernel, shapes, [ANY] * 4, (ANY, VMEM, VMEM), scratch)(*in_far(queries, grad_output, keys, values))


def chain(parents_ref, level, seg):
    found = []
    current = seg
    for upper in range(level - 1, -1, -1):
        current = parents_ref[upper, current]
        found.insert(0, current)
    return found


def tile_at(upper, ancestor):
    return pl.ds(pl.multiple_of((upper * SEGS + ancestor) * TILE, TILE), TILE)


def rows_of(level, seg, first, count):
    return pl.ds((level * SEGS + seg) * PIECE + first, count)


def select_kernel(parents_ref, held_ref, out_ref, wide, picked):
    wide[0 : DEVICES * TILE] = held_ref[...].astype(jnp.float32)

    def step(seg, carry):
        for upper, ancestor in enumerate(chain(parents_ref, 3, seg)):
            tile = wide[tile_at(upper, ancestor), :]
            picked[rows_of(3, seg, 4 * upper, 4), :] = tile[0:4]
            picked[rows_of(0, seg, 4 * upper, 4), :] = tile[4:8]
        first, second = [wide[tile_at(u, a), :] for u, a in enumerate(chain(parents_ref, 2, seg))]
        picked[rows_of(2, seg, 0, 4), :] = first[0:4]
        picked[rows_of(2, seg, 4, 4), :] = second[0:4]
        picked[rows_of(2, seg, 8, 2), :] = first[4:6]
        picked[rows_of(2, seg, 10, 2), :] = second[4:6]
        picked[rows_of(1, seg, 8, 2), :] = first[6:8]
        picked[rows_of(1, seg, 10, 2), :] = second[6:8]
        (only,) = chain(parents_ref, 1, seg)
        picked[rows_of(1, seg, 0, 8), :] = wide[tile_at(0, only), :]
        return carry

    lax.fori_loop(0, SEGS, step, 0, unroll=True)
    out_ref[...] = picked[0 : DEVICES * PIECE].astype(jnp.bfloat16)


def select(parents, held):
    scratch = [wide_scratch(DEVICES * TILE), wide_scratch(DEVICES * PIECE)]
    return call(select_kernel, near(DEVICES * PIECE, HD), [SMEM, VMEM], VMEM, scratch)(parents, held)


def sum_kernel(parents_ref, terms_ref, after_ref, out_ref, wide, *totals):
    wide[0 : DEVICES * PIECE] = terms_ref[...].astype(jnp.float32)
    for total in totals:
        total[...] = jnp.zeros_like(total)
    from_three, from_two, from_one = totals[:3], totals[3:5], totals[5]

    def rows(level, seg, first, count):
        return wide[rows_of(level, seg, first, count), :]

    def step(seg, carry):
        for upper, ancestor in enumerate(chain(parents_ref, 3, seg)):
            from_three[upper][tile_at(0, ancestor), :] += jnp.concatenate(
                [rows(3, seg, 4 * upper, 4), rows(0, seg, 4 * upper, 4)]
            )
        for upper, ancestor in enumerate(chain(parents_ref, 2, seg)):
            from_two[upper][tile_at(0, ancestor), :] += jnp.concatenate(
                [rows(2, seg, 4 * upper, 4), rows(2, seg, 8 + 2 * upper, 2), rows(1, seg, 8 + 2 * upper, 2)]
            )
        (only,) = chain(parents_ref, 1, seg)
        from_one[tile_at(0, only), :] += rows(1, seg, 0, 8)
        return carry

    lax.fori_loop(0, SEGS, step, 0, unroll=True)
    size = SEGS * TILE
    out_ref[0:size] = (from_three[0][...] + from_two[0][...] + from_one[...]).astype(jnp.bfloat16)
    out_ref[size : 2 * size] = (from_three[1][...] + from_two[1][...]).astype(jnp.bfloat16)
    out_ref[2 * size : 3 * size] = from_three[2][...].astype(jnp.bfloat16)
    out_ref[3 * size :] = jnp.zeros((size, HD), jnp.bfloat16)


def sum_terms(parents, terms, after):
    scratch = [wide_scratch(DEVICES * PIECE)] + [near(SEGS * TILE, HD, dtype=jnp.float32)] * 6
    return call(sum_kernel, near(DEVICES * TILE, HD), [SMEM, VMEM, ANY], VMEM, scratch)(
        parents, *in_near(terms), after
    )


def dot_last(left, right):
    return lax.dot_general(left, right, (((1,), (1,)), ((), ())), preferred_element_type=jnp.float32)


def dot(left, right):
    return jnp.dot(left, right, preferred_element_type=jnp.float32)


def block_mask(lengths):
    slots = lax.broadcasted_iota(jnp.int32, (ROWS, ROWS), 0)
    rows = lax.broadcasted_iota(jnp.int32, (ROWS, ROWS), 1)
    allowed = [slots < length for length in lengths]
    allowed[-1] = allowed[-1] & (slots <= rows)
    return jnp.concatenate([jnp.where(each, 0.0, -jnp.inf).astype(jnp.float32) for each in allowed])


def head_grad(keys, values, blocked, live_rows, query_at, grad_at, store):
    query = jnp.concatenate([query_at(i) for i in range(REPEAT)])
    grad = jnp.concatenate(
        [jnp.where(live_rows, grad_at(i), jnp.zeros((), jnp.bfloat16)) for i in range(REPEAT)]
    )
    scores = dot_last(keys, query) * (FACTOR * LOG2E) + jnp.concatenate([blocked] * REPEAT, axis=1)
    weights = jnp.exp2(scores - jnp.max(scores, axis=0, keepdims=True))
    probs = weights * (1.0 / jnp.sum(weights, axis=0, keepdims=True))
    grad_probs = dot_last(values, grad)
    correction = jnp.sum(probs * grad_probs, axis=0, keepdims=True)
    grad_scores = (probs * ((grad_probs - correction) * FACTOR)).astype(jnp.bfloat16)
    value_sum = dot(probs.astype(jnp.bfloat16), grad)
    key_sum = dot(grad_scores, query)
    turned = dot(keys.T, grad_scores).astype(jnp.bfloat16)
    for i in range(REPEAT):
        store(i, turned[:, i * ROWS : (i + 1) * ROWS].T)
    return key_sum, value_sum


def live(length):
    return lax.broadcasted_iota(jnp.int32, (ROWS, HD), 0) < length


def lanes_at(ref, start, width=HD):
    return ref.at[:, start : start + width]


def root_kernel(
    place_ref, lengths_ref, query_ref, grad_ref, key_ref, value_ref, first_ref, second_ref, after_ref, picked_ref,
    gquery_ref, gkey_ref, gvalue_ref, query_tasks, grad_tasks, key_tasks, value_tasks,
    query, grad, keys, values, gquery, sems, task_sems,
):
    def fetches(level, index):
        guest, head, _ = TASKS[level][index]
        if guest:
            wide_at, narrow_at = (head - HALF) * GROUP, HALF * GROUP + (head - HALF) * HD
            many = (first_ref, second_ref, first_ref, second_ref)
        else:
            wide_at, narrow_at = head * GROUP, head * HD
            many = (query_ref, grad_ref, key_ref, value_ref)
        copies = [
            pltpu.make_async_copy(lanes_at(ref, narrow_at), target.at[index], task_sems.at[index, i])
            for i, (ref, target) in enumerate(zip(many[2:], (key_tasks, value_tasks)))
        ]
        if index in EARLY[level]:
            position = EARLY[level].index(index)
            copies += [
                pltpu.make_async_copy(lanes_at(ref, wide_at, GROUP), target.at[position], task_sems.at[index, 2 + i])
                for i, (ref, target) in enumerate(zip(many[:2], (query_tasks, grad_tasks)))
            ]
        return copies

    def gather(level):
        copies = [copy for index in range(len(TASKS[level])) for copy in fetches(level, index)]
        for copy in copies:
            copy.start()
        for copy in copies:
            copy.wait()

    for level in range(LEVELS):
        pl.when(place_ref[0] == level)(lambda level=level: gather(level))

    @pl.when(place_ref[0] == 0)
    def _():
        pairs = ((query_ref, query), (grad_ref, grad), (key_ref, keys), (value_ref, values))
        copies = [pltpu.make_async_copy(*pair, sems.at[i]) for i, pair in enumerate(pairs)]
        for copy in copies:
            copy.start()
        for copy in copies:
            copy.wait()
        length = lengths_ref[0, place_ref[1]]
        blocked = block_mask([length])
        for head in range(HEADS):
            lanes = slice(head * HD, (head + 1) * HD)

            def store(i, block):
                lanes_at(gquery, head * GROUP + i * HD)[...] = block

            gkey_ref[:, lanes], gvalue_ref[:, lanes] = head_grad(
                keys[:, lanes],
                values[:, lanes],
                blocked,
                live(length),
                lambda i: lanes_at(query, head * GROUP + i * HD)[...],
                lambda i: lanes_at(grad, head * GROUP + i * HD)[...],
                store,
            )
        out = pltpu.make_async_copy(gquery, gquery_ref, sems.at[0])
        out.start()
        out.wait()


def task_shapes():
    return near(2, ROWS, GROUP), near(2, ROWS, GROUP), near(MOST, ROWS, HD), near(MOST, ROWS, HD)


def root_grad(place, lengths, queries, grad_output, keys, values, first, second, *after):
    shapes = (
        far(ROWS, HEADS * GROUP), far(ROWS, WIDTH, dtype=jnp.float32), far(ROWS, WIDTH, dtype=jnp.float32),
    ) + task_shapes()
    specs = [SMEM, SMEM] + [ANY] * 8
    outs = (ANY,) + (VMEM,) * 6
    scratch = [
        near(ROWS, HEADS * GROUP), near(ROWS, HEADS * GROUP), near(ROWS, WIDTH), near(ROWS, WIDTH),
        near(ROWS, HEADS * GROUP), pltpu.SemaphoreType.DMA((4,)), pltpu.SemaphoreType.DMA((MOST, 4)),
    ]
    return call(root_kernel, shapes, specs, outs, scratch, flops=10**9, moved=6 * 2**20)(
        place, lengths, *in_far(queries, grad_output, keys, values), first, second, *after
    )


def attention_kernel(
    place_ref, parents_ref, lengths_ref, query_ref, grad_ref, query, grad, keys, values, held,
    gquery_ref, gkey_ref, gvalue_ref, back_ref, terms_ref,
    late_query, late_grad, gquery, gkey, gvalue, back_own, wide, sums, terms_low, in_sems, out_sems, own_sems,
):
    level_here = place_ref[0]
    seg = place_ref[1]

    def result(level, index):
        guest, head, _ = TASKS[level][index]
        target = lanes_at(back_ref, (head - HALF) * GROUP, GROUP) if guest else lanes_at(gquery_ref, head * GROUP, GROUP)
        return pltpu.make_async_copy(gquery.at[index], target, out_sems.at[index])

    def at_level(level, body):
        pl.when(level_here == level)(body)

    def late(level, index):
        place, start = LATE[level].index(index), TASKS[level][index][1] * GROUP
        return [
            pltpu.make_async_copy(lanes_at(ref, start, GROUP), target.at[place], in_sems.at[place, i])
            for i, (ref, target) in enumerate(((query_ref, late_query), (grad_ref, late_grad)))
        ]

    def fetch_late(level):
        for index in LATE[level]:
            for copy in late(level, index):
                copy.start()

    for level in (1, 2):
        at_level(level, lambda level=level: fetch_late(level))
    wide[0 : ROWS * PIECE] = held[...].astype(jnp.float32)

    def slot_rows(slot, part):
        return pl.ds(2 * slot + part, ROWS, stride=PIECE)

    def setting(level):
        lengths = [lengths_ref[u, a] for u, a in enumerate(chain(parents_ref, level, seg))]
        lengths.append(lengths_ref[level, seg])
        return block_mask(lengths), live(lengths[-1])

    def work(level, index, blocked, live_rows):
        slots = TASKS[level][index][2]
        key_list, value_list = [
            jnp.concatenate([wide[slot_rows(slot, part), :].astype(jnp.bfloat16) for slot in slots] + [mine[index]])
            for part, mine in enumerate((keys, values))
        ]

        if index in EARLY[level]:
            place, query_from, grad_from = EARLY[level].index(index), query, grad
        else:
            place, query_from, grad_from = LATE[level].index(index), late_query, late_grad

        def store(i, block):
            gquery[index, :, i * HD : (i + 1) * HD] = block

        key_sum, value_sum = head_grad(
            key_list,
            value_list,
            blocked,
            live_rows,
            lambda i: query_from[place, :, i * HD : (i + 1) * HD],
            lambda i: grad_from[place, :, i * HD : (i + 1) * HD],
            store,
        )
        for position, slot in enumerate(slots):
            block = slice(position * ROWS, (position + 1) * ROWS)
            sums[slot_rows(slot, 0), :] = key_sum[block]
            sums[slot_rows(slot, 1), :] = value_sum[block]
        gkey[index] = key_sum[len(slots) * ROWS :]
        gvalue[index] = value_sum[len(slots) * ROWS :]

    def work_on(level, indices, *settings):
        for index in indices:
            if index in LATE[level]:
                for copy in late(level, index):
                    copy.wait()
        for index, (blocked, live_rows) in zip(indices, settings):
            work(level, index, blocked, live_rows)

    def send(level, indices):
        for index in indices:
            result(level, index).start()

    @pl.when((level_here == 3) | (level_here == 0))
    def _():
        work_on(3, (0, 1), *[setting(3)] * 2)
        at_level(3, lambda: send(3, (0, 1)))
        at_level(0, lambda: send(0, (0, 1)))

    @pl.when(level_here == 2)
    def _():
        both = setting(2)
        work_on(2, (0, 1), both, both)
        send(2, (0, 1))
        work_on(2, (2,), both)
        send(2, (2,))

    @pl.when(level_here == 1)
    def _():
        own, other = setting(1), setting(2)
        work_on(1, (4, 0), other, own)
        send(1, (4, 0))
        work_on(1, (1, 2, 3), own, own, own)
        send(1, (1, 2, 3))

    terms_low[...] = sums[0 : ROWS * PIECE].astype(jnp.bfloat16)
    terms_out = pltpu.make_async_copy(terms_low, terms_ref, own_sems.at[0])
    terms_out.start()

    def hand_out(level):
        copies = []
        for index, (guest, head, _) in enumerate(TASKS[level]):
            if guest:
                place = head - HALF
                back_own[:, place * HD : (place + 1) * HD] = gkey[index].astype(jnp.bfloat16)
                back_own[:, (HALF + place) * HD : (HALF + place + 1) * HD] = gvalue[index].astype(jnp.bfloat16)
            else:
                for i, (source, target) in enumerate(((gkey, gkey_ref), (gvalue, gvalue_ref))):
                    copies.append(
                        pltpu.make_async_copy(source.at[index], lanes_at(target, head * HD), in_sems.at[index, i])
                    )
        if level in HOST:
            copies.append(pltpu.make_async_copy(back_own, lanes_at(back_ref, BACK_KEY, 2 * HALF * HD), own_sems.at[1]))
        for copy in copies:
            copy.start()
        for copy in copies + [result(level, index) for index in range(len(TASKS[level]))]:
            copy.wait()

    for level in range(LEVELS):
        at_level(level, lambda level=level: hand_out(level))
    terms_out.wait()


def attention(place, parents, lengths, queries, grad_output, tasks, held):
    shapes = (
        far(ROWS, HEADS * GROUP), far(ROWS, WIDTH, dtype=jnp.float32), far(ROWS, WIDTH, dtype=jnp.float32),
        far(ROWS, BACK_VALUE + HALF * HD), far(ROWS * PIECE, HD),
    )
    specs = [SMEM] * 3 + [ANY] * 2 + [VMEM] * 5
    outs = (ANY,) * 5
    scratch = [
        near(MOST, ROWS, GROUP),
        near(MOST, ROWS, GROUP),
        near(MOST, ROWS, GROUP),
        near(MOST, ROWS, HD, dtype=jnp.float32),
        near(MOST, ROWS, HD, dtype=jnp.float32),
        near(ROWS, 2 * HALF * HD),
        wide_scratch(ROWS * PIECE),
        wide_scratch(ROWS * PIECE),
        near(ROWS * PIECE, HD),
        pltpu.SemaphoreType.DMA((MOST, 2)),
        pltpu.SemaphoreType.DMA((MOST,)),
        pltpu.SemaphoreType.DMA((2,)),
    ]
    return call(attention_kernel, shapes, specs, outs, scratch, flops=3 * 10**9, moved=10 * 2**20)(
        place, parents, lengths, *in_far(queries, grad_output), *in_near(*tasks, held)
    )


def token_kernel(after_ref, out_ref):
    out_ref[...] = jnp.zeros_like(out_ref)


def token(after):
    return call(token_kernel, full(8, HD), [ANY], VMEM, flops=BESIDE)(after)


def join_kernel(
    place_ref, root_ref, here_ref, back_ref, root_key_ref, here_key_ref, back_key_ref,
    root_value_ref, here_value_ref, back_value_ref, out_ref, key_ref, value_ref,
):
    level = place_ref[0]
    head = pl.program_id(0)
    away = ((level == 3) & (head >= HALF)) | ((level == 2) & (head == HEADS - 1))

    def take(source, key_source, value_source):
        out_ref[...] = source[...]
        key_ref[...] = key_source[...].astype(jnp.float32)
        value_ref[...] = value_source[...].astype(jnp.float32)

    pl.when(away)(lambda: take(back_ref, back_key_ref, back_value_ref))
    pl.when(level == 0)(lambda: take(root_ref, root_key_ref, root_value_ref))
    pl.when((level != 0) & jnp.logical_not(away))(lambda: take(here_ref, here_key_ref, here_value_ref))


def join(place, root, here, back):
    def spec(width, skipped, first):
        return pl.BlockSpec((ROWS, width), lambda h: (0, first // width + jnp.maximum(h - skipped, 0)))

    root, here, operands, specs = in_far(*root), in_far(*here), [place], [SMEM]
    for index, (width, first) in enumerate(((GROUP, 0), (HD, BACK_KEY), (HD, BACK_VALUE))):
        operands += [root[index], here[index], back]
        specs += [spec(width, 0, 0), spec(width, 0, 0), spec(width, HALF, first)]
    shapes = (low(ROWS, HEADS * GROUP), full(ROWS, WIDTH), full(ROWS, WIDTH))
    outs = (spec(GROUP, 0, 0), spec(HD, 0, 0), spec(HD, 0, 0))
    return call(join_kernel, shapes, specs, outs, grid=(HEADS,), moved=6 * 2**20)(*operands)


def finish_kernel(extra_ref, own_key_ref, own_value_ref, key_ref, value_ref, wide):
    wide[0 : ROWS * TILE] = extra_ref[...].astype(jnp.float32)
    for head in range(HEADS):
        lanes = slice(head * HD, (head + 1) * HD)
        for part, (own_ref, out_ref) in enumerate(((own_key_ref, key_ref), (own_value_ref, value_ref))):
            extra = wide[pl.ds(2 * head + part, ROWS, stride=TILE), :]
            out_ref[:, lanes] = (own_ref[:, lanes] + extra).astype(jnp.bfloat16)


def finish(extra, own_key, own_value):
    shapes = (low(ROWS, WIDTH), low(ROWS, WIDTH))
    return call(finish_kernel, shapes, [VMEM] * 3, (VMEM, VMEM), [wide_scratch(ROWS * TILE)])(
        extra, own_key, own_value
    )


def exchange(pieces, *tile):
    rows = pieces.shape[0]
    swapped = lax.all_to_all(pieces.reshape(DEVICES, *tile, HD), ("depth", "seg"), 0, 0, tiled=True)
    return swapped.reshape(rows, HD)


def per_device(queries, key_states, value_states, grad_output, parents, lengths):
    place = jnp.stack([lax.axis_index("depth"), lax.axis_index("seg")]).astype(jnp.int32)
    place, parents, lengths = [pltpu.with_memory_space_constraint(x, pltpu.SMEM) for x in (place, parents, lengths)]
    packed, *lent = pack(queries, grad_output, key_states, value_states)
    first, second = [lax.ppermute(each, "depth", [(host, here) for here, host in HOST.items()]) for each in lent]
    picked = select(parents, exchange(packed, TILE))
    arrived = exchange(picked, SLOTS // 2, 4)
    *root, query_tasks, grad_tasks, key_tasks, value_tasks = root_grad(
        place, lengths, queries, grad_output, key_states, value_states, first, second, token(first), picked
    )
    tasks = (query_tasks, grad_tasks, key_tasks, value_tasks)
    *here, back, terms = attention(place, parents, lengths, queries, grad_output, tasks, arrived)
    back = lax.ppermute(back, "depth", list(HOST.items()))
    grad_q, own_k, own_v = join(place, root, here, back)
    extra = exchange(sum_terms(parents, exchange(terms, SLOTS // 2, 4), token(back)), TILE)
    grad_k, grad_v = finish(extra, own_k, own_v)
    return grad_q, grad_k, grad_v


def solution(mesh):
    placed = P(("depth", "seg"), "tp")
    return jax.shard_map(
        per_device,
        mesh=mesh,
        in_specs=(placed, placed, placed, placed, P(), P()),
        out_specs=(placed, placed, placed),
        check_vma=False,
    )
```

```python
import jax
import jax.numpy as jnp
from jax import lax
from jax.experimental import pallas as pl
from jax.experimental.pallas import tpu as pltpu
from jax.sharding import PartitionSpec as P

HD = 128
LEVELS = 4
SEGS = 32
ROWS = 128
HEADS = 4
REPEAT = 8
GROUP = REPEAT * HD
WIDTH = HEADS * HD
TILE = 2 * HEADS
UPPER = LEVELS - 1
DEVICES = LEVELS * SEGS
SLOTS = 6
PIECE = 2 * SLOTS
HALF = HEADS // 2
LENT = HALF * (GROUP + HD)
BACK_KEY = HALF * GROUP
BACK_VALUE = BACK_KEY + HALF * HD
VMEM_LIMIT = 32 * 1024 * 1024
BESIDE = 4 * 10**10
LOG2E = 1.4426950408889634
FACTOR = HD ** (-0.5)
VMEM = pl.BlockSpec(memory_space=pltpu.VMEM)
SMEM = pl.BlockSpec(memory_space=pltpu.SMEM)
ANY = pl.BlockSpec(memory_space=pl.ANY)

TASKS = {
    0: ((True, 2, (0, 2, 4)), (True, 3, (1, 3, 5))),
    1: ((False, 0, (0,)), (False, 1, (1,)), (False, 2, (2,)), (False, 3, (3,)), (True, 3, (4, 5))),
    2: ((False, 0, (0, 2)), (False, 1, (1, 3)), (False, 2, (4, 5))),
    3: ((False, 0, (0, 2, 4)), (False, 1, (1, 3, 5))),
}
HOST = {0: 3, 1: 2}
EARLY = {0: (0, 1), 1: (4, 0), 2: (0, 1), 3: (0, 1)}
LATE = {0: (), 1: (1, 2, 3), 2: (2,), 3: ()}
MOST = max(len(tasks) for tasks in TASKS.values())


def call(kernel, out_shape, in_specs, out_specs, scratch=(), flops=0, moved=0, grid=None):
    extra = {} if grid is None else {"grid": grid}
    return pl.pallas_call(
        kernel,
        out_shape=out_shape,
        in_specs=in_specs,
        out_specs=out_specs,
        scratch_shapes=list(scratch),
        cost_estimate=pl.CostEstimate(flops=flops, bytes_accessed=moved, transcendentals=0),
        compiler_params=pltpu.CompilerParams(vmem_limit_bytes=VMEM_LIMIT),
        **extra,
    )


def low(*shape):
    return jax.ShapeDtypeStruct(shape, jnp.bfloat16)


def full(*shape):
    return jax.ShapeDtypeStruct(shape, jnp.float32)


def near(*shape, dtype=jnp.bfloat16):
    return pltpu.VMEM(shape, dtype)


def far(*shape, dtype=jnp.bfloat16):
    return pltpu.HBM(shape, dtype)


def in_far(*arrays):
    return [pltpu.with_memory_space_constraint(array, pltpu.HBM) for array in arrays]


def in_near(*arrays):
    return [pltpu.with_memory_space_constraint(array, pltpu.VMEM) for array in arrays]


def wide_scratch(rows):
    return pltpu.VMEM((rows + 16, HD), jnp.float32)


def pack_kernel(
    query_ref, grad_ref, key_ref, value_ref, out_ref, first_ref, second_ref, keys, values, packed, wide, sems
):
    half = HALF * GROUP
    copies = [
        pltpu.make_async_copy(key_ref, keys, sems.at[0]),
        pltpu.make_async_copy(value_ref, values, sems.at[1]),
        pltpu.make_async_copy(query_ref.at[:, half:], first_ref.at[:, :half], sems.at[2]),
        pltpu.make_async_copy(grad_ref.at[:, half:], second_ref.at[:, :half], sems.at[3]),
    ]
    for copy in copies:
        copy.start()
    for copy in copies[:2]:
        copy.wait()
    for head in range(HEADS):
        lanes = slice(head * HD, (head + 1) * HD)
        wide[pl.ds(2 * head, ROWS, stride=TILE), :] = keys[:, lanes].astype(jnp.float32)
        wide[pl.ds(2 * head + 1, ROWS, stride=TILE), :] = values[:, lanes].astype(jnp.float32)
    packed[...] = wide[0 : ROWS * TILE].astype(jnp.bfloat16)
    out = pltpu.make_async_copy(packed, out_ref, sems.at[0])
    out.start()
    first_ref[:, half:] = keys[:, HALF * HD :]
    second_ref[:, half:] = values[:, HALF * HD :]
    for copy in copies[2:] + [out]:
        copy.wait()


def pack(queries, grad_output, keys, values):
    shapes = (far(ROWS * TILE, HD), near(ROWS, LENT), near(ROWS, LENT))
    scratch = [near(ROWS, WIDTH), near(ROWS, WIDTH), near(ROWS * TILE, HD), wide_scratch(ROWS * TILE)]
    scratch.append(pltpu.SemaphoreType.DMA((4,)))
    return call(pack_kernel, shapes, [ANY] * 4, (ANY, VMEM, VMEM), scratch)(*in_far(queries, grad_output, keys, values))


def chain(parents_ref, level, seg):
    found = []
    current = seg
    for upper in range(level - 1, -1, -1):
        current = parents_ref[upper, current]
        found.insert(0, current)
    return found


def tile_at(upper, ancestor):
    return pl.ds(pl.multiple_of((upper * SEGS + ancestor) * TILE, TILE), TILE)


def rows_of(level, seg, first, count):
    return pl.ds((level * SEGS + seg) * PIECE + first, count)


def select_kernel(parents_ref, held_ref, out_ref, wide, picked):
    wide[0 : DEVICES * TILE] = held_ref[...].astype(jnp.float32)

    def step(seg, carry):
        for upper, ancestor in enumerate(chain(parents_ref, 3, seg)):
            tile = wide[tile_at(upper, ancestor), :]
            picked[rows_of(3, seg, 4 * upper, 4), :] = tile[0:4]
            picked[rows_of(0, seg, 4 * upper, 4), :] = tile[4:8]
        first, second = [wide[tile_at(u, a), :] for u, a in enumerate(chain(parents_ref, 2, seg))]
        picked[rows_of(2, seg, 0, 4), :] = first[0:4]
        picked[rows_of(2, seg, 4, 4), :] = second[0:4]
        picked[rows_of(2, seg, 8, 2), :] = first[4:6]
        picked[rows_of(2, seg, 10, 2), :] = second[4:6]
        picked[rows_of(1, seg, 8, 2), :] = first[6:8]
        picked[rows_of(1, seg, 10, 2), :] = second[6:8]
        (only,) = chain(parents_ref, 1, seg)
        picked[rows_of(1, seg, 0, 8), :] = wide[tile_at(0, only), :]
        return carry

    lax.fori_loop(0, SEGS, step, 0, unroll=True)
    out_ref[...] = picked[0 : DEVICES * PIECE].astype(jnp.bfloat16)


def select(parents, held):
    scratch = [wide_scratch(DEVICES * TILE), wide_scratch(DEVICES * PIECE)]
    return call(select_kernel, near(DEVICES * PIECE, HD), [SMEM, VMEM], VMEM, scratch)(parents, held)


def sum_kernel(parents_ref, terms_ref, after_ref, out_ref, wide, *totals):
    wide[0 : DEVICES * PIECE] = terms_ref[...].astype(jnp.float32)
    for total in totals:
        total[...] = jnp.zeros_like(total)
    from_three, from_two, from_one = totals[:3], totals[3:5], totals[5]

    def rows(level, seg, first, count):
        return wide[rows_of(level, seg, first, count), :]

    def step(seg, carry):
        for upper, ancestor in enumerate(chain(parents_ref, 3, seg)):
            from_three[upper][tile_at(0, ancestor), :] += jnp.concatenate(
                [rows(3, seg, 4 * upper, 4), rows(0, seg, 4 * upper, 4)]
            )
        for upper, ancestor in enumerate(chain(parents_ref, 2, seg)):
            from_two[upper][tile_at(0, ancestor), :] += jnp.concatenate(
                [rows(2, seg, 4 * upper, 4), rows(2, seg, 8 + 2 * upper, 2), rows(1, seg, 8 + 2 * upper, 2)]
            )
        (only,) = chain(parents_ref, 1, seg)
        from_one[tile_at(0, only), :] += rows(1, seg, 0, 8)
        return carry

    lax.fori_loop(0, SEGS, step, 0, unroll=True)
    size = SEGS * TILE
    out_ref[0:size] = (from_three[0][...] + from_two[0][...] + from_one[...]).astype(jnp.bfloat16)
    out_ref[size : 2 * size] = (from_three[1][...] + from_two[1][...]).astype(jnp.bfloat16)
    out_ref[2 * size : 3 * size] = from_three[2][...].astype(jnp.bfloat16)
    out_ref[3 * size :] = jnp.zeros((size, HD), jnp.bfloat16)


def sum_terms(parents, terms, after):
    scratch = [wide_scratch(DEVICES * PIECE)] + [near(SEGS * TILE, HD, dtype=jnp.float32)] * 6
    return call(sum_kernel, near(DEVICES * TILE, HD), [SMEM, VMEM, ANY], VMEM, scratch)(
        parents, *in_near(terms), after
    )


def dot_last(left, right):
    return lax.dot_general(left, right, (((1,), (1,)), ((), ())), preferred_element_type=jnp.float32)


def dot(left, right):
    return jnp.dot(left, right, preferred_element_type=jnp.float32)


def block_mask(lengths):
    slots = lax.broadcasted_iota(jnp.int32, (ROWS, ROWS), 0)
    rows = lax.broadcasted_iota(jnp.int32, (ROWS, ROWS), 1)
    allowed = [slots < length for length in lengths]
    allowed[-1] = allowed[-1] & (slots <= rows)
    return jnp.concatenate([jnp.where(each, 0.0, -jnp.inf).astype(jnp.float32) for each in allowed])


def head_grad(keys, values, blocked, live_rows, query_at, grad_at, store):
    query = jnp.concatenate([query_at(i) for i in range(REPEAT)])
    grad = jnp.concatenate(
        [jnp.where(live_rows, grad_at(i), jnp.zeros((), jnp.bfloat16)) for i in range(REPEAT)]
    )
    scores = dot_last(keys, query) * (FACTOR * LOG2E) + jnp.concatenate([blocked] * REPEAT, axis=1)
    weights = jnp.exp2(scores - jnp.max(scores, axis=0, keepdims=True))
    probs = weights * (1.0 / jnp.sum(weights, axis=0, keepdims=True))
    grad_probs = dot_last(values, grad)
    correction = jnp.sum(probs * grad_probs, axis=0, keepdims=True)
    grad_scores = (probs * (grad_probs - correction)).astype(jnp.bfloat16)
    value_sum = dot(probs.astype(jnp.bfloat16), grad)
    key_sum = dot(grad_scores, query) * FACTOR
    turned = (dot(keys.T, grad_scores) * FACTOR).astype(jnp.bfloat16)
    for i in range(REPEAT):
        store(i, turned[:, i * ROWS : (i + 1) * ROWS].T)
    return key_sum, value_sum


def live(length):
    return lax.broadcasted_iota(jnp.int32, (ROWS, HD), 0) < length


def lanes_at(ref, start, width=HD):
    return ref.at[:, start : start + width]


def root_kernel(
    place_ref, lengths_ref, query_ref, grad_ref, key_ref, value_ref, first_ref, second_ref, after_ref, picked_ref,
    gquery_ref, gkey_ref, gvalue_ref, query_tasks, grad_tasks, key_tasks, value_tasks,
    query, grad, keys, values, gquery, sems, task_sems,
):
    def fetches(level, index):
        guest, head, _ = TASKS[level][index]
        if guest:
            wide_at, narrow_at = (head - HALF) * GROUP, HALF * GROUP + (head - HALF) * HD
            many = (first_ref, second_ref, first_ref, second_ref)
        else:
            wide_at, narrow_at = head * GROUP, head * HD
            many = (query_ref, grad_ref, key_ref, value_ref)
        copies = [
            pltpu.make_async_copy(lanes_at(ref, narrow_at), target.at[index], task_sems.at[index, i])
            for i, (ref, target) in enumerate(zip(many[2:], (key_tasks, value_tasks)))
        ]
        if index in EARLY[level]:
            position = EARLY[level].index(index)
            copies += [
                pltpu.make_async_copy(lanes_at(ref, wide_at, GROUP), target.at[position], task_sems.at[index, 2 + i])
                for i, (ref, target) in enumerate(zip(many[:2], (query_tasks, grad_tasks)))
            ]
        return copies

    def gather(level):
        copies = [copy for index in range(len(TASKS[level])) for copy in fetches(level, index)]
        for copy in copies:
            copy.start()
        for copy in copies:
            copy.wait()

    for level in range(LEVELS):
        pl.when(place_ref[0] == level)(lambda level=level: gather(level))

    @pl.when(place_ref[0] == 0)
    def _():
        pairs = ((query_ref, query), (grad_ref, grad), (key_ref, keys), (value_ref, values))
        copies = [pltpu.make_async_copy(*pair, sems.at[i]) for i, pair in enumerate(pairs)]
        for copy in copies:
            copy.start()
        for copy in copies:
            copy.wait()
        length = lengths_ref[0, place_ref[1]]
        blocked = block_mask([length])
        for head in range(HEADS):
            lanes = slice(head * HD, (head + 1) * HD)

            def store(i, block):
                lanes_at(gquery, head * GROUP + i * HD)[...] = block

            gkey_ref[:, lanes], gvalue_ref[:, lanes] = head_grad(
                keys[:, lanes],
                values[:, lanes],
                blocked,
                live(length),
                lambda i: lanes_at(query, head * GROUP + i * HD)[...],
                lambda i: lanes_at(grad, head * GROUP + i * HD)[...],
                store,
            )
        out = pltpu.make_async_copy(gquery, gquery_ref, sems.at[0])
        out.start()
        out.wait()


def task_shapes():
    return near(2, ROWS, GROUP), near(2, ROWS, GROUP), near(MOST, ROWS, HD), near(MOST, ROWS, HD)


def root_grad(place, lengths, queries, grad_output, keys, values, first, second, *after):
    shapes = (
        far(ROWS, HEADS * GROUP), far(ROWS, WIDTH, dtype=jnp.float32), far(ROWS, WIDTH, dtype=jnp.float32),
    ) + task_shapes()
    specs = [SMEM, SMEM] + [ANY] * 8
    outs = (ANY,) + (VMEM,) * 6
    scratch = [
        near(ROWS, HEADS * GROUP), near(ROWS, HEADS * GROUP), near(ROWS, WIDTH), near(ROWS, WIDTH),
        near(ROWS, HEADS * GROUP), pltpu.SemaphoreType.DMA((4,)), pltpu.SemaphoreType.DMA((MOST, 4)),
    ]
    return call(root_kernel, shapes, specs, outs, scratch, flops=10**9, moved=6 * 2**20)(
        place, lengths, *in_far(queries, grad_output, keys, values), first, second, *after
    )


def attention_kernel(
    place_ref, parents_ref, lengths_ref, query_ref, grad_ref, query, grad, keys, values, held,
    gquery_ref, gkey_ref, gvalue_ref, back_ref, terms_ref,
    late_query, late_grad, gquery, gkey, gvalue, back_own, wide, sums, terms_low, in_sems, out_sems, own_sems,
):
    level_here = place_ref[0]
    seg = place_ref[1]

    def result(level, index):
        guest, head, _ = TASKS[level][index]
        target = lanes_at(back_ref, (head - HALF) * GROUP, GROUP) if guest else lanes_at(gquery_ref, head * GROUP, GROUP)
        return pltpu.make_async_copy(gquery.at[index], target, out_sems.at[index])

    def at_level(level, body):
        pl.when(level_here == level)(body)

    def late(level, index):
        place, start = LATE[level].index(index), TASKS[level][index][1] * GROUP
        return [
            pltpu.make_async_copy(lanes_at(ref, start, GROUP), target.at[place], in_sems.at[place, i])
            for i, (ref, target) in enumerate(((query_ref, late_query), (grad_ref, late_grad)))
        ]

    def fetch_late(level):
        for index in LATE[level]:
            for copy in late(level, index):
                copy.start()

    for level in (1, 2):
        at_level(level, lambda level=level: fetch_late(level))
    wide[0 : ROWS * PIECE] = held[...].astype(jnp.float32)

    def slot_rows(slot, part):
        return pl.ds(2 * slot + part, ROWS, stride=PIECE)

    def setting(level):
        lengths = [lengths_ref[u, a] for u, a in enumerate(chain(parents_ref, level, seg))]
        lengths.append(lengths_ref[level, seg])
        return block_mask(lengths), live(lengths[-1])

    def work(level, index, blocked, live_rows):
        slots = TASKS[level][index][2]
        key_list, value_list = [
            jnp.concatenate([wide[slot_rows(slot, part), :].astype(jnp.bfloat16) for slot in slots] + [mine[index]])
            for part, mine in enumerate((keys, values))
        ]

        if index in EARLY[level]:
            place, query_from, grad_from = EARLY[level].index(index), query, grad
        else:
            place, query_from, grad_from = LATE[level].index(index), late_query, late_grad

        def store(i, block):
            gquery[index, :, i * HD : (i + 1) * HD] = block

        key_sum, value_sum = head_grad(
            key_list,
            value_list,
            blocked,
            live_rows,
            lambda i: query_from[place, :, i * HD : (i + 1) * HD],
            lambda i: grad_from[place, :, i * HD : (i + 1) * HD],
            store,
        )
        for position, slot in enumerate(slots):
            block = slice(position * ROWS, (position + 1) * ROWS)
            sums[slot_rows(slot, 0), :] = key_sum[block]
            sums[slot_rows(slot, 1), :] = value_sum[block]
        gkey[index] = key_sum[len(slots) * ROWS :]
        gvalue[index] = value_sum[len(slots) * ROWS :]

    def work_on(level, indices, *settings):
        for index in indices:
            if index in LATE[level]:
                for copy in late(level, index):
                    copy.wait()
        for index, (blocked, live_rows) in zip(indices, settings):
            work(level, index, blocked, live_rows)

    def send(level, indices):
        for index in indices:
            result(level, index).start()

    @pl.when((level_here == 3) | (level_here == 0))
    def _():
        work_on(3, (0, 1), *[setting(3)] * 2)
        at_level(3, lambda: send(3, (0, 1)))
        at_level(0, lambda: send(0, (0, 1)))

    @pl.when(level_here == 2)
    def _():
        both = setting(2)
        work_on(2, (0, 1), both, both)
        send(2, (0, 1))
        work_on(2, (2,), both)
        send(2, (2,))

    @pl.when(level_here == 1)
    def _():
        own, other = setting(1), setting(2)
        work_on(1, (4, 0), other, own)
        send(1, (4, 0))
        work_on(1, (1, 2), own, own)
        send(1, (1, 2))
        work_on(1, (3,), own)
        send(1, (3,))

    terms_low[...] = sums[0 : ROWS * PIECE].astype(jnp.bfloat16)
    terms_out = pltpu.make_async_copy(terms_low, terms_ref, own_sems.at[0])
    terms_out.start()

    def hand_out(level):
        copies = []
        for index, (guest, head, _) in enumerate(TASKS[level]):
            if guest:
                place = head - HALF
                back_own[:, place * HD : (place + 1) * HD] = gkey[index].astype(jnp.bfloat16)
                back_own[:, (HALF + place) * HD : (HALF + place + 1) * HD] = gvalue[index].astype(jnp.bfloat16)
            else:
                for i, (source, target) in enumerate(((gkey, gkey_ref), (gvalue, gvalue_ref))):
                    copies.append(
                        pltpu.make_async_copy(source.at[index], lanes_at(target, head * HD), in_sems.at[index, i])
                    )
        if level in HOST:
            copies.append(pltpu.make_async_copy(back_own, lanes_at(back_ref, BACK_KEY, 2 * HALF * HD), own_sems.at[1]))
        for copy in copies:
            copy.start()
        for copy in copies + [result(level, index) for index in range(len(TASKS[level]))]:
            copy.wait()

    for level in range(LEVELS):
        at_level(level, lambda level=level: hand_out(level))
    terms_out.wait()


def attention(place, parents, lengths, queries, grad_output, tasks, held):
    shapes = (
        far(ROWS, HEADS * GROUP), far(ROWS, WIDTH, dtype=jnp.float32), far(ROWS, WIDTH, dtype=jnp.float32),
        far(ROWS, BACK_VALUE + HALF * HD), far(ROWS * PIECE, HD),
    )
    specs = [SMEM] * 3 + [ANY] * 2 + [VMEM] * 5
    outs = (ANY,) * 5
    scratch = [
        near(MOST, ROWS, GROUP),
        near(MOST, ROWS, GROUP),
        near(MOST, ROWS, GROUP),
        near(MOST, ROWS, HD, dtype=jnp.float32),
        near(MOST, ROWS, HD, dtype=jnp.float32),
        near(ROWS, 2 * HALF * HD),
        wide_scratch(ROWS * PIECE),
        wide_scratch(ROWS * PIECE),
        near(ROWS * PIECE, HD),
        pltpu.SemaphoreType.DMA((MOST, 2)),
        pltpu.SemaphoreType.DMA((MOST,)),
        pltpu.SemaphoreType.DMA((2,)),
    ]
    return call(attention_kernel, shapes, specs, outs, scratch, flops=3 * 10**9, moved=10 * 2**20)(
        place, parents, lengths, *in_far(queries, grad_output), *in_near(*tasks, held)
    )


def token_kernel(after_ref, out_ref):
    out_ref[...] = jnp.zeros_like(out_ref)


def token(after):
    return call(token_kernel, full(8, HD), [ANY], VMEM, flops=BESIDE)(after)


def join_kernel(
    place_ref, root_ref, here_ref, back_ref, root_key_ref, here_key_ref, back_key_ref,
    root_value_ref, here_value_ref, back_value_ref, out_ref, key_ref, value_ref,
):
    level = place_ref[0]
    head = pl.program_id(0)
    away = ((level == 3) & (head >= HALF)) | ((level == 2) & (head == HEADS - 1))

    def take(source, key_source, value_source):
        out_ref[...] = source[...]
        key_ref[...] = key_source[...].astype(jnp.float32)
        value_ref[...] = value_source[...].astype(jnp.float32)

    pl.when(away)(lambda: take(back_ref, back_key_ref, back_value_ref))
    pl.when(level == 0)(lambda: take(root_ref, root_key_ref, root_value_ref))
    pl.when((level != 0) & jnp.logical_not(away))(lambda: take(here_ref, here_key_ref, here_value_ref))


def join(place, root, here, back):
    def spec(width, skipped, first):
        return pl.BlockSpec((ROWS, width), lambda h: (0, first // width + jnp.maximum(h - skipped, 0)))

    root, here, operands, specs = in_far(*root), in_far(*here), [place], [SMEM]
    for index, (width, first) in enumerate(((GROUP, 0), (HD, BACK_KEY), (HD, BACK_VALUE))):
        operands += [root[index], here[index], back]
        specs += [spec(width, 0, 0), spec(width, 0, 0), spec(width, HALF, first)]
    shapes = (low(ROWS, HEADS * GROUP), full(ROWS, WIDTH), full(ROWS, WIDTH))
    outs = (spec(GROUP, 0, 0), spec(HD, 0, 0), spec(HD, 0, 0))
    return call(join_kernel, shapes, specs, outs, grid=(HEADS,), moved=6 * 2**20)(*operands)


def finish_kernel(extra_ref, own_key_ref, own_value_ref, key_ref, value_ref, wide):
    wide[0 : ROWS * TILE] = extra_ref[...].astype(jnp.float32)
    for head in range(HEADS):
        lanes = slice(head * HD, (head + 1) * HD)
        for part, (own_ref, out_ref) in enumerate(((own_key_ref, key_ref), (own_value_ref, value_ref))):
            extra = wide[pl.ds(2 * head + part, ROWS, stride=TILE), :]
            out_ref[:, lanes] = (own_ref[:, lanes] + extra).astype(jnp.bfloat16)


def finish(extra, own_key, own_value):
    shapes = (low(ROWS, WIDTH), low(ROWS, WIDTH))
    return call(finish_kernel, shapes, [VMEM] * 3, (VMEM, VMEM), [wide_scratch(ROWS * TILE)])(
        extra, own_key, own_value
    )


def exchange(pieces, *tile):
    rows = pieces.shape[0]
    swapped = lax.all_to_all(pieces.reshape(DEVICES, *tile, HD), ("depth", "seg"), 0, 0, tiled=True)
    return swapped.reshape(rows, HD)


def per_device(queries, key_states, value_states, grad_output, parents, lengths):
    place = jnp.stack([lax.axis_index("depth"), lax.axis_index("seg")]).astype(jnp.int32)
    place, parents, lengths = [pltpu.with_memory_space_constraint(x, pltpu.SMEM) for x in (place, parents, lengths)]
    packed, *lent = pack(queries, grad_output, key_states, value_states)
    first, second = [lax.ppermute(each, "depth", [(host, here) for here, host in HOST.items()]) for each in lent]
    picked = select(parents, exchange(packed, TILE))
    arrived = exchange(picked, SLOTS // 2, 4)
    *root, query_tasks, grad_tasks, key_tasks, value_tasks = root_grad(
        place, lengths, queries, grad_output, key_states, value_states, first, second, token(first), picked
    )
    tasks = (query_tasks, grad_tasks, key_tasks, value_tasks)
    *here, back, terms = attention(place, parents, lengths, queries, grad_output, tasks, arrived)
    back = lax.ppermute(back, "depth", list(HOST.items()))
    grad_q, own_k, own_v = join(place, root, here, back)
    extra = exchange(sum_terms(parents, exchange(terms, SLOTS // 2, 4), token(back)), TILE)
    grad_k, grad_v = finish(extra, own_k, own_v)
    return grad_q, grad_k, grad_v


def solution(mesh):
    placed = P(("depth", "seg"), "tp")
    return jax.shard_map(
        per_device,
        mesh=mesh,
        in_specs=(placed, placed, placed, placed, P(), P()),
        out_specs=(placed, placed, placed),
        check_vma=False,
    )
```
